32 devices in a mesh: wide: 8 (over y, x, core), narrow: 4 (over z).
Axes of the slice: x: 2, y: 2, z: 4, core: 2. Of those that a mesh axis runs over, the one named last changes fastest.
Arguments:
- block_in: bfloat16 [2, 4096, 1280], P(None, ('wide', 'narrow')), may hold values from -6 to 6
- cotangent: bfloat16 [2, 4096, 1280], P(None, ('wide', 'narrow')), may hold values from -6 to 6
- routes: int32 [2, 4096, 7], P(None, ('wide', 'narrow')), may hold values from 0 to 14, all different within a row; in each aligned block of 128 rows (0 to 127, 128 to 255, ..., all dimensions but the last counted through in order) at most 64 rows name the same one
- seq_ids: int32 [2, 4096], P(None, ('wide', 'narrow')), may hold values from 0 to 127, as said below
- slot_order: int32 [16], replicated, may hold values from 0 to 15, each once
- attention_in: float32 [1280, 3840], P(('wide', 'narrow')), may hold values from -0.15625 to 0.15625
- attention_in_moment: float32 [1280, 3840], P(('wide', 'narrow'))
- attention_in_average: float32 [1280, 3840], P(('wide', 'narrow')), may hold values from -0.15625 to 0.15625
- attention_out: float32 [1280, 1280], P(('wide', 'narrow')), may hold values from -0.625 to 0.625
- attention_out_moment: float32 [1280, 1280], P(('wide', 'narrow'))
- attention_out_average: float32 [1280, 1280], P(('wide', 'narrow')), may hold values from -0.625 to 0.625
- shared_in: float32 [1280, 1792], P(('wide', 'narrow')), may hold values from -0.15625 to 0.15625
- shared_in_moment: float32 [1280, 1792], P(('wide', 'narrow'))
- shared_in_average: float32 [1280, 1792], P(('wide', 'narrow')), may hold values from -0.15625 to 0.15625
- shared_out: float32 [896, 1280], P(None, ('wide', 'narrow')), may hold values from -0.1875 to 0.1875
- shared_out_moment: float32 [896, 1280], P(None, ('wide', 'narrow'))
- shared_out_average: float32 [896, 1280], P(None, ('wide', 'narrow')), may hold values from -0.1875 to 0.1875
- router: float32 [1280, 15], P(('wide', 'narrow')), may hold values from -0.078125 to 0.078125
- router_moment: float32 [1280, 15], P(('wide', 'narrow'))
- router_average: float32 [1280, 15], P(('wide', 'narrow')), may hold values from -0.078125 to 0.078125
- gains: float32 [2, 1280], P(None, ('wide', 'narrow')), may hold values from 0.5 to 1.5
- gains_moment: float32 [2, 1280], P(None, ('wide', 'narrow'))
- gains_average: float32 [2, 1280], P(None, ('wide', 'narrow')), may hold values from 0.5 to 1.5
- experts_in: float32 [16, 1280, 1792], P('narrow', 'wide'), may hold values from -0.15625 to 0.15625
- experts_in_moment: float32 [16, 1280, 1792], P('narrow', 'wide')
- experts_in_average: float32 [16, 1280, 1792], P('narrow', 'wide'), may hold values from -0.15625 to 0.15625
- experts_out: float32 [16, 896, 1280], P('narrow', None, 'wide'), may hold values from -2 to 2
- experts_out_moment: float32 [16, 896, 1280], P('narrow', None, 'wide')
- experts_out_average: float32 [16, 896, 1280], P('narrow', None, 'wide'), may hold values from -2 to 2
Outputs:
- block_out: bfloat16 [2, 4096, 1280], P(None, ('wide', 'narrow'))
- input_grad: bfloat16 [2, 4096, 1280], P(None, ('wide', 'narrow'))
- attention_in_momentum: float32 [1280, 3840], P(('wide', 'narrow'))
- attention_out_momentum: float32 [1280, 1280], P(('wide', 'narrow'))
- shared_in_momentum: float32 [1280, 1792], P(('wide', 'narrow'))
- shared_out_momentum: float32 [896, 1280], P(None, ('wide', 'narrow'))
- router_momentum: float32 [1280, 15], P(('wide', 'narrow'))
- gains_momentum: float32 [2, 1280], P(None, ('wide', 'narrow'))
- experts_in_momentum: float32 [16, 1280, 1792], P('narrow', 'wide')
- experts_out_momentum: float32 [16, 896, 1280], P('narrow', None, 'wide')
- attention_in_state: float32 [2, 1280, 3840], P(None, ('wide', 'narrow'))
- attention_out_state: float32 [2, 1280, 1280], P(None, ('wide', 'narrow'))
- shared_in_state: float32 [2, 1280, 1792], P(None, ('wide', 'narrow'))
- shared_out_state: float32 [2, 896, 1280], P(None, None, ('wide', 'narrow'))
- router_state: float32 [2, 1280, 15], P(None, ('wide', 'narrow'))
- gains_state: float32 [2, 2, 1280], P(None, None, ('wide', 'narrow'))
- experts_in_state: float32 [2, 16, 1280, 1792], P(None, 'narrow', 'wide')
- experts_out_state: float32 [2, 16, 896, 1280], P(None, 'narrow', None, 'wide')
The draws below stay inside these ranges and needn't reach their ends.
Inputs may be any that keep to these rules, and one draw needn't show every extreme that they name: `routes`: each row names 7 different routed experts; among the rows of one device in one microbatch (aligned blocks of 128) no expert is named by more than 64 rows, a bound that some block reaches. A permutation of the slots: routed expert e sits in slot slot_order[e]; the slot in the last entry holds no expert. `seq_ids`: within each row of 128 tokens, a token's entry is the index in that row of the first token of its sequence; the first token of a row has 0, and in the first row of each microbatch the last token starts a sequence of its own.
All inputs are finite; a program needn't handle non-finite values.
Results may differ from the reference program's by a relative error of at most 0.018.
Values may be sent and summed in bfloat16 or wider, within the bound.
No kernel may reach another device: no remote copies, remote signals or barrier semaphores. Data moves between devices by JAX's collectives and lax.ppermute only.
A program may use at most 320 MiB of HBM per device.

```python
import math
import jax
import jax.numpy as jnp
import numpy as np
from jax import lax

D = 1280
HEADS = 10
HEAD_DIM = 128
SH_FF = 896
EXP_FF = 896
TOPK = 7
MB = 2
MB_TOK = 128
SLOTS = 16
ROUTED = 15
NTOK = 4096
TOKENS = 8192
CAP = 64


def moment_draw(key, shape, spread):
    return spread * jax.random.normal(key, shape, jnp.float32)


def draw_seq_ids(key, part):
    marks = jax.random.randint(key, (MB, NTOK // MB_TOK, MB_TOK), 0, 128)
    positions = jnp.arange(MB_TOK, dtype=jnp.int32)
    row_ids = jnp.arange(NTOK // MB_TOK, dtype=jnp.int32)[None, :, None]
    forced = (row_ids == 0) & (positions == MB_TOK - 1)
    starts = jnp.where((marks == 0) | (positions == 0) | forced, positions, 0).astype(jnp.int32)
    return lax.cummax(starts, axis=2).reshape(MB, NTOK).astype(jnp.int32)


def draw_attention_in_moment(key, part):
    return moment_draw(key, (D, 3 * D), 2.0 * math.sqrt(TOKENS))


def draw_attention_out_moment(key, part):
    return moment_draw(key, (D, D), 0.5 * math.sqrt(TOKENS))


def draw_shared_in_moment(key, part):
    return moment_draw(key, (D, 2 * SH_FF), 1.4 * math.sqrt(TOKENS))


def draw_shared_out_moment(key, part):
    return moment_draw(key, (SH_FF, D), 1.2 * math.sqrt(TOKENS))


def draw_router_moment(key, part):
    return moment_draw(key, (D, ROUTED), 30.0 * math.sqrt(TOKENS))


def draw_gains_moment(key, part):
    return moment_draw(key, (2, D), 4.0 * math.sqrt(TOKENS))


def draw_experts_in_moment(key, part):
    return moment_draw(key, (SLOTS, D, 2 * EXP_FF), math.sqrt(TOKENS * TOPK / ROUTED))


def draw_experts_out_moment(key, part):
    return moment_draw(key, (SLOTS, EXP_FF, D), 1.2 / ROUTED * math.sqrt(TOKENS * TOPK / ROUTED))


def level_of(rng, dims, cuts, low, largest):
    loudness, own = 1.0, jax.random.fold_in(rng, 6)
    for position, shards_of in cuts:
        heights = jnp.exp(jax.random.uniform(jax.random.fold_in(own, position), (shards_of,), jnp.float32, low / len(cuts), largest / len(cuts)))
        loudness = loudness * jnp.repeat(heights, dims[position] // shards_of).reshape([-1 if axis == position else 1 for axis in range(len(dims))])
    return loudness


def assign_block(stream_key, own, number, rows, count, top, limit, lean):
    ranking = jax.random.permutation(stream_key, count)
    crowded, usual = load_shares(count, rows * top, limit, lean, True), load_shares(count, rows * top, limit, lean, False)
    places = jnp.arange(count)

    def named(sizes, rotation):
        used = int((sizes > 0).sum())
        fixed = max(1, used // 4)
        shifted = fixed + (places - fixed + rotation * (used - fixed)) % max(1, count - fixed)
        return jnp.zeros((count,), jnp.int32).at[ranking[jnp.where(places < fixed, places, shifted)]].set(jnp.asarray(sizes, jnp.int32))

    sizes = jnp.where(number % 4 == 0, named(crowded, number // 4), named(usual, number - number // 4 - 1))
    mixed = jax.random.permutation(jax.random.fold_in(own, 3), count)
    giver, receiver = mixed[0:count // 2 * 2:2], mixed[1:count // 2 * 2:2]
    slack = jnp.minimum(sizes[giver] - 1, limit - sizes[receiver]) // 2
    slack = jnp.where((giver == ranking[0]) | (receiver == ranking[0]) | (sizes[receiver] == 0), 0, jnp.maximum(slack, 0))
    shifted = jax.random.randint(jax.random.fold_in(own, 4), (count // 2,), 0, 1 << 20) % (slack + 1)
    sizes = sizes.at[giver].add(-shifted).at[receiver].add(shifted)
    items = jnp.searchsorted(jnp.cumsum(sizes), jnp.arange(rows * top), side="right").astype(jnp.int32)
    table = items.reshape(top, rows).T
    table = table[jax.random.permutation(jax.random.fold_in(own, 1), rows)]
    rotation = jax.random.randint(jax.random.fold_in(own, 2), (rows, 1), 0, top)
    return jnp.take_along_axis(table, (jnp.arange(top)[None, :] + rotation) % top, axis=1)


def load_shares(number_of, total, reach, slope, full):
    loads = [(1 << 20) // math.isqrt(standing ** slope) + 1 for standing in range(1, number_of + 1)]
    largest = reach if full else min(reach, max(-(-total // number_of), total * loads[0] // sum(loads)))
    least = 1 if total - largest >= number_of - 1 else 0
    holding, surplus = [largest] + [least] * (number_of - 1), total - largest - least * (number_of - 1)
    while surplus > 0:
        movable = [i for i in range(1, number_of) if holding[i] < largest] or [i for i in range(1, number_of) if holding[i] < reach]
        whole, budget = sum([loads[i] for i in movable]), surplus
        for i in movable:
            extra = min(reach - holding[i], max(1, budget * loads[i] // whole), surplus)
            holding[i] = holding[i] + extra
            surplus = surplus - extra
    return np.array(holding)


def bell_draw(own_key, extent, scale, bound, cuts=(), kind=jnp.bfloat16):
    result = scale * jax.random.normal(own_key, extent, jnp.float32)
    if cuts:
        result = result * level_of(own_key, extent, cuts, -0.22, 0.18)
    return jnp.clip(result, -bound, bound).astype(kind)


def setup_inputs(seed: int = 0) -> dict:
    key_of = jax.random.split(jax.random.key(seed), 30)
    block_in = bell_draw(key_of[0], (MB, NTOK, D), 1.0, 6.0, ((1, 32),))
    cotangent = bell_draw(key_of[1], (MB, NTOK, D), 1.0, 6.0, ((1, 32),))
    routes_keys = jax.random.split(jax.random.fold_in(key_of[2], 1), MB * NTOK // MB_TOK)
    routes_turns = jax.random.permutation(jax.random.fold_in(key_of[2], 3), MB * NTOK // MB_TOK)
    routes = jax.vmap(lambda own, number: assign_block(jax.random.fold_in(key_of[2], 2), own, number, MB_TOK, ROUTED, TOPK, CAP, 1))(routes_keys, routes_turns).reshape((MB, NTOK, TOPK))
    seq_ids = draw_seq_ids(jax.random.fold_in(key_of[29], 71), 0)
    slot_order = jax.random.permutation(key_of[4], SLOTS).astype(jnp.int32)
    attention_in = bell_draw(key_of[5], (D, 3 * D), D ** -0.5, 0.15625, ((0, 32),), jnp.float32)
    attention_in_moment = draw_attention_in_moment(jax.random.fold_in(key_of[29], 71), 0)
    attention_in_average = bell_draw(key_of[7], (D, 3 * D), D ** -0.5, 0.15625, ((0, 32),), jnp.float32)
    attention_out = bell_draw(key_of[8], (D, D), (D // 16) ** -0.5, 0.625, ((0, 32),), jnp.float32)
    attention_out_moment = draw_attention_out_moment(jax.random.fold_in(key_of[29], 71), 0)
    attention_out_average = bell_draw(key_of[10], (D, D), (D // 16) ** -0.5, 0.625, ((0, 32),), jnp.float32)
    shared_in = bell_draw(key_of[11], (D, 2 * SH_FF), D ** -0.5, 0.15625, ((0, 32),), jnp.float32)
    shared_in_moment = draw_shared_in_moment(jax.random.fold_in(key_of[29], 71), 0)
    shared_in_average = bell_draw(key_of[13], (D, 2 * SH_FF), D ** -0.5, 0.15625, ((0, 32),), jnp.float32)
    shared_out = bell_draw(key_of[14], (SH_FF, D), SH_FF ** -0.5, 0.1875, ((1, 32),), jnp.float32)
    shared_out_moment = draw_shared_out_moment(jax.random.fold_in(key_of[29], 71), 0)
    shared_out_average = bell_draw(key_of[16], (SH_FF, D), SH_FF ** -0.5, 0.1875, ((1, 32),), jnp.float32)
    router = bell_draw(key_of[17], (D, ROUTED), (4 * D) ** -0.5, 0.078125, ((0, 32),), jnp.float32)
    router_moment = draw_router_moment(jax.random.fold_in(key_of[29], 71), 0)
    router_average = bell_draw(key_of[19], (D, ROUTED), (4 * D) ** -0.5, 0.078125, ((0, 32),), jnp.float32)
    gains = jnp.clip(1.0 + 0.1 * jax.random.normal(key_of[20], (2, D), jnp.float32), 0.5, 1.5)
    gains_moment = draw_gains_moment(jax.random.fold_in(key_of[29], 71), 0)
    gains_average = jnp.clip(1.0 + 0.1 * jax.random.normal(key_of[22], (2, D), jnp.float32), 0.5, 1.5)
    experts_in = bell_draw(key_of[23], (SLOTS, D, 2 * EXP_FF), D ** -0.5, 0.15625, ((0, 4), (1, 8)), jnp.float32)
    experts_in_moment = draw_experts_in_moment(jax.random.fold_in(key_of[29], 71), 0)
    experts_in_average = bell_draw(key_of[25], (SLOTS, D, 2 * EXP_FF), D ** -0.5, 0.15625, ((0, 4), (1, 8)), jnp.float32)
    experts_out = bell_draw(key_of[26], (SLOTS, EXP_FF, D), (max(1, EXP_FF * 5 // (2 * SLOTS * SLOTS))) ** -0.5, 2.0, ((0, 4), (2, 8)), jnp.float32)
    experts_out_moment = draw_experts_out_moment(jax.random.fold_in(key_of[29], 71), 0)
    experts_out_average = bell_draw(key_of[28], (SLOTS, EXP_FF, D), (max(1, EXP_FF * 5 // (2 * SLOTS * SLOTS))) ** -0.5, 2.0, ((0, 4), (2, 8)), jnp.float32)
    return dict(block_in=block_in, cotangent=cotangent, routes=routes, seq_ids=seq_ids, slot_order=slot_order, attention_in=attention_in, attention_in_moment=attention_in_moment, attention_in_average=attention_in_average, attention_out=attention_out, attention_out_moment=attention_out_moment, attention_out_average=attention_out_average, shared_in=shared_in, shared_in_moment=shared_in_moment, shared_in_average=shared_in_average, shared_out=shared_out, shared_out_moment=shared_out_moment, shared_out_average=shared_out_average, router=router, router_moment=router_moment, router_average=router_average, gains=gains, gains_moment=gains_moment, gains_average=gains_average, experts_in=experts_in, experts_in_moment=experts_in_moment, experts_in_average=experts_in_average, experts_out=experts_out, experts_out_moment=experts_out_moment, experts_out_average=experts_out_average)


HIGHEST = lax.Precision.HIGHEST
EPSILON = 1e-06
MOMENTUM_DECAY = 0.9
AVERAGE_DECAY = 0.99
STEP_RATES = (0.006, 0.1, 0.009, 0.0125, 0.0002, 0.011, 0.027, 8.0)
MASKED = -1e+30

@jax.custom_vjp
def low(v):
    return lax.optimization_barrier(v.astype(jnp.bfloat16)).astype(jnp.float32)

@jax.custom_vjp
def low_back(v):
    return v

def low_keep(v):
    return (low(v), None)

def low_pass(kept, grad):
    return (grad,)

def back_keep(v):
    return (v, None)

def back_low(kept, grad):
    return (low(grad),)
low.defvjp(low_keep, low_pass)
low_back.defvjp(back_keep, back_low)

def rms_scale(rows_in):
    return lax.rsqrt(lax.optimization_barrier(jnp.mean(rows_in * rows_in, axis=-1, keepdims=True)) + EPSILON)

def rotary_tables(positions):
    half_dim = HEAD_DIM // 2
    freqs = jnp.exp(jnp.arange(half_dim, dtype=jnp.float32) * (-2.0 * math.log(10000.0) / HEAD_DIM))
    angles = positions.astype(jnp.float32)[..., None] * freqs
    return (jnp.cos(angles)[..., None, :], jnp.sin(angles)[..., None, :])

def rotate(vectors, cosines, sines):
    half_dim = vectors.shape[-1] // 2
    first_half = vectors[..., :half_dim]
    second_half = vectors[..., half_dim:]
    return jnp.concatenate([first_half * cosines - second_half * sines, second_half * cosines + first_half * sines], axis=-1)

def attend_row(pieces):
    queries, keys_rot, values, doc_starts = pieces
    positions = jnp.arange(MB_TOK, dtype=jnp.int32)
    allowed = (doc_starts[:, None] == doc_starts[None, :]) & (positions[None, :] <= positions[:, None])
    scores = jnp.einsum('qhd,khd->hqk', queries, keys_rot, precision=HIGHEST) * HEAD_DIM ** (-0.5)
    scores = jnp.where(allowed[None], low_back(scores), MASKED)
    probs_row = jax.nn.softmax(scores, axis=-1)
    return jnp.einsum('hqk,khd->qhd', low(probs_row), values, precision=HIGHEST)

def forward(rows_in, flat_routes, doc_rows, slot_order, attention_in, attention_out, shared_in, shared_out, router, gains, experts_in, experts_out):
    gain_rows = low(gains)
    first_norm = low(rows_in * rms_scale(rows_in) * gain_rows[0])
    projected = low_back(jnp.dot(first_norm, low(attention_in), precision=HIGHEST))
    projected = projected.reshape(-1, MB_TOK, 3, HEADS, HEAD_DIM)
    positions = jnp.arange(MB_TOK, dtype=jnp.int32)[None, :] - doc_rows
    cosines, sines = rotary_tables(positions)
    queries = low(rotate(projected[:, :, 0], cosines, sines))
    keys_rot = low(rotate(projected[:, :, 1], cosines, sines))
    values = low(projected[:, :, 2])
    attended = lax.map(jax.checkpoint(attend_row), (queries, keys_rot, values, doc_rows))
    attended = low_back(low(attended)).reshape(-1, D)
    hidden = rows_in + low_back(jnp.dot(attended, low(attention_out), precision=HIGHEST))
    second_norm = low(hidden * rms_scale(hidden) * gain_rows[1])
    shared_pre = low_back(jnp.dot(second_norm, low(shared_in), precision=HIGHEST))
    shared_act = low(jax.nn.silu(shared_pre[:, :SH_FF]) * shared_pre[:, SH_FF:])
    shared_branch = jnp.dot(shared_act, low(shared_out), precision=HIGHEST)
    logits = jnp.dot(second_norm, low(router), precision=HIGHEST)
    router_probs = jax.nn.softmax(logits, axis=-1)
    chosen = lax.optimization_barrier(jnp.sum((flat_routes[:, :, None] == jnp.arange(ROUTED, dtype=jnp.int32)).astype(jnp.float32), axis=1))
    shares = (router_probs * chosen).T
    owners = slot_order[:ROUTED]
    expert_in = low(experts_in)[owners]
    expert_out = low(experts_out)[owners]

    def expert_step(running, pieces):
        weight_in, weight_out, share_col = pieces
        expert_rows = low_back(second_norm)
        pre_act = low_back(jnp.dot(expert_rows, weight_in, precision=HIGHEST))
        activated = low(jax.nn.silu(pre_act[:, :EXP_FF]) * pre_act[:, EXP_FF:])
        produced = low_back(low(jnp.dot(activated, weight_out, precision=HIGHEST)))
        return (running + share_col[:, None] * produced, None)
    running, unused = lax.scan(jax.checkpoint(expert_step), jnp.zeros_like(rows_in), (expert_in, expert_out, shares))
    return hidden + shared_branch + running

def reference(block_in, cotangent, routes, seq_ids, slot_order, attention_in, attention_in_moment, attention_in_average, attention_out, attention_out_moment, attention_out_average, shared_in, shared_in_moment, shared_in_average, shared_out, shared_out_moment, shared_out_average, router, router_moment, router_average, gains, gains_moment, gains_average, experts_in, experts_in_moment, experts_in_average, experts_out, experts_out_moment, experts_out_average):
    flat_routes = routes.reshape(-1, TOPK)
    doc_rows = seq_ids.reshape(-1, MB_TOK)
    masters = (attention_in, attention_out, shared_in, shared_out, router, gains, experts_in, experts_out)
    moments = (attention_in_moment, attention_out_moment, shared_in_moment, shared_out_moment, router_moment, gains_moment, experts_in_moment, experts_out_moment)
    averages = (attention_in_average, attention_out_average, shared_in_average, shared_out_average, router_average, gains_average, experts_in_average, experts_out_average)

    def run(rows_in, attention_in, attention_out, shared_in, shared_out, router, gains, experts_in, experts_out):
        return forward(rows_in, flat_routes, doc_rows, slot_order, attention_in, attention_out, shared_in, shared_out, router, gains, experts_in, experts_out)
    outputs, pull_back = jax.vjp(run, block_in.astype(jnp.float32).reshape(-1, D), attention_in, attention_out, shared_in, shared_out, router, gains, experts_in, experts_out)
    grads_all = pull_back(cotangent.astype(jnp.float32).reshape(-1, D))
    block_out = outputs.reshape(MB, -1, D).astype(jnp.bfloat16)
    input_grad = grads_all[0].reshape(MB, -1, D).astype(jnp.bfloat16)
    base_rate = 1.0 / math.sqrt(TOKENS)
    moment_outs = []
    states = []
    for master, moment, average, grad_share, step_rate in zip(masters, moments, averages, grads_all[1:], STEP_RATES):
        moment_new = MOMENTUM_DECAY * moment + grad_share
        master_new = master - step_rate * base_rate * (grad_share + MOMENTUM_DECAY * moment_new)
        average_new = AVERAGE_DECAY * average + (1.0 - AVERAGE_DECAY) * master_new
        moment_outs.append(moment_new)
        states.append(jnp.stack([average_new, master_new]))
    return (block_out, input_grad, moment_outs[0], moment_outs[1], moment_outs[2], moment_outs[3], moment_outs[4], moment_outs[5], moment_outs[6], moment_outs[7], states[0], states[1], states[2], states[3], states[4], states[5], states[6], states[7])
```

```python
import math

import jax
import jax.numpy as jnp
from jax import lax
from jax.sharding import PartitionSpec as P

D = 1280
HEADS = 10
HEAD_DIM = 128
FF = 896
TOPK = 7
EXP_DEV = 4
MB = 2
MB_TOK = 128
LANES = 128

HIGHEST = lax.Precision.HIGHEST
EPSILON = 1e-06
MOMENTUM_DECAY = 0.9
AVERAGE_DECAY = 0.99
STEP_RATES = (0.006, 0.1, 0.009, 0.0125, 0.0002, 0.011, 0.027, 8.0)
MASKED = -1e30

ECOLS = 3 * FF
ACOLS = 4 * D + LANES
bfloat = jnp.bfloat16
single = jnp.float32


def split_cols(cols):
    return (cols // LANES + 1) // 2 * LANES


def dot(a, b, dims=(((1,), (0,)), ((), ()))):
    return lax.dot_general(a, b, dims, preferred_element_type=single)


NT = (((1,), (1,)), ((), ()))
TN = (((0,), (0,)), ((), ()))


def rms_scale(rows_in):
    return lax.rsqrt(jnp.mean(rows_in * rows_in, axis=-1, keepdims=True) + EPSILON)


def norm_back(rows_in, scale_rows, gain_row, grad_norm):
    normed = rows_in * scale_rows
    weighted = grad_norm * gain_row
    grad_rows = scale_rows * (
        weighted - normed * jnp.mean(weighted * normed, axis=-1, keepdims=True)
    )
    return (grad_rows, jnp.sum(grad_norm * normed, axis=0))


def rotary_tables(positions):
    half_dim = HEAD_DIM // 2
    freqs = jnp.exp(jnp.arange(half_dim, dtype=jnp.float32) * (-2.0 * math.log(10000.0) / HEAD_DIM))
    angles = positions.astype(jnp.float32)[..., None] * freqs
    return (jnp.cos(angles)[..., None, :], jnp.sin(angles)[..., None, :])


def rotate(vectors, cosines, sines):
    half_dim = vectors.shape[-1] // 2
    first_half = vectors[..., :half_dim]
    second_half = vectors[..., half_dim:]
    return jnp.concatenate(
        [first_half * cosines - second_half * sines, second_half * cosines + first_half * sines],
        axis=-1,
    )


def swiglu(gate_pre, up_pre):
    return gate_pre * jax.nn.sigmoid(gate_pre) * up_pre


def swiglu_back(gate_pre, up_pre, grad_act):
    sigmoid_gate = jax.nn.sigmoid(gate_pre)
    grad_gate = grad_act * up_pre * sigmoid_gate * (1.0 + gate_pre * (1.0 - sigmoid_gate))
    grad_up = grad_act * gate_pre * sigmoid_gate
    return (grad_gate, grad_up)


def wide_xor(piece, bit):
    count = lax.axis_size("wide")
    return lax.ppermute(piece, "wide", [(i, i ^ bit) for i in range(count)])


def ring(piece):
    count = lax.axis_size("narrow")
    return lax.ppermute(piece, "narrow", [(i, (i + 1) % count) for i in range(count)])


def chip_bits():
    bits, bit = [], 2
    while bit < lax.axis_size("wide"):
        bits.append(bit)
        bit *= 2
    return bits


def gather_plane(shard):
    cut = split_cols(shard.shape[1])
    halves = []
    for part, order in (
        (shard[:, :cut], chip_bits()),
        (shard[:, cut:], chip_bits()[::-1]),
    ):
        pieces = {0: part}
        for bit in order:
            pieces.update({r | bit: wide_xor(p, bit) for r, p in list(pieces.items())})
        pieces.update({r | 1: wide_xor(p, 1) for r, p in list(pieces.items())})
        halves.append(pieces)
    return [(halves[0][r], halves[1][r]) for r in range(lax.axis_size("wide"))]


def assemble(pieces):
    me = lax.axis_index("wide")
    rows, cut = pieces[0][0].shape
    full = jnp.zeros((len(pieces) * rows, cut + pieces[0][1].shape[1]), bfloat)
    for r, (left, right) in enumerate(pieces):
        full = lax.dynamic_update_slice(full, left, ((me ^ r) * rows, 0))
        full = lax.dynamic_update_slice(full, right, ((me ^ r) * rows, cut))
    return full


def place(pieces):
    level = lax.axis_index("narrow")
    count = len(pieces)
    full = jnp.zeros((count, *pieces[0].shape), pieces[0].dtype)
    for s, piece in enumerate(pieces):
        full = lax.dynamic_update_index_in_dim(full, piece, (level - s) % count, 0)
    return full


def scatter_plane(full):
    wide_count = lax.axis_size("wide")
    me = lax.axis_index("wide")
    rows = full.shape[0] // wide_count
    view = full.astype(bfloat).reshape(wide_count // 2, 2, rows, full.shape[1])
    core = me & 1
    give = lax.dynamic_index_in_dim(view, 1 - core, axis=1, keepdims=False)
    keep = lax.dynamic_index_in_dim(view, core, axis=1, keepdims=False)
    total = keep.astype(single) + wide_xor(give, 1).astype(single)
    cut = split_cols(full.shape[1])
    parts = []
    bit_count = len(chip_bits())
    for part, order in (
        (total[..., :cut], list(range(bit_count))[::-1]),
        (total[..., cut:], list(range(bit_count))),
    ):
        blocks = part.astype(bfloat)
        present = list(range(bit_count))
        for bit_index in order:
            give, keep = halves(blocks, present.index(bit_index), (me >> (bit_index + 1)) & 1)
            present.remove(bit_index)
            summed = keep.astype(single) + wide_xor(give, 2 << bit_index).astype(single)
            blocks = summed.astype(bfloat)
        parts.append(summed[0])
    return jnp.concatenate(parts, axis=1)


def halves(blocks, place, own):
    count = blocks.shape[0]
    low = 1 << place
    view = blocks.reshape(count // (2 * low), 2, low, *blocks.shape[1:])
    give = lax.dynamic_index_in_dim(view, 1 - own, axis=1, keepdims=False)
    keep = lax.dynamic_index_in_dim(view, own, axis=1, keepdims=False)
    shape = (count // 2, *blocks.shape[1:])
    return give.reshape(shape), keep.reshape(shape)


def ring_gather(piece):
    pieces = [piece]
    for _ in range(lax.axis_size("narrow") - 1):
        pieces.append(ring(pieces[-1]))
    return pieces


def ring_scatter(block_of):
    count = lax.axis_size("narrow")
    total = block_of(1).astype(bfloat)
    for step in range(1, count):
        arrived = ring(total)
        last = step == count - 1
        total = arrived.astype(single) + block_of((step + 1) % count).astype(single)
        if not last:
            total = total.astype(bfloat)
    return total


def local(
    block_in,
    cotangent,
    routes,
    seq_ids,
    slot_order,
    attention_in,
    attention_in_moment,
    attention_in_average,
    attention_out,
    attention_out_moment,
    attention_out_average,
    shared_in,
    shared_in_moment,
    shared_in_average,
    shared_out,
    shared_out_moment,
    shared_out_average,
    router,
    router_moment,
    router_average,
    gains,
    gains_moment,
    gains_average,
    experts_in,
    experts_in_moment,
    experts_in_average,
    experts_out,
    experts_out_moment,
    experts_out_average,
):
    wide_count = lax.axis_size("wide")
    narrow_count = lax.axis_size("narrow")
    level = lax.axis_index("narrow")
    slots = EXP_DEV * narrow_count
    routed = slots - 1
    capacity = (MB_TOK * TOPK * 8 // (7 * slots) + 7) // 8 * 8
    tokens = MB * MB_TOK * wide_count * narrow_count
    own_tokens = MB * MB_TOK
    rows_dense = D // (wide_count * narrow_count)
    rows_plane = D // wide_count
    blocks = MB * narrow_count
    quarter = FF // narrow_count
    shared_width = (quarter + LANES - 1) // LANES * LANES

    pad_small = jnp.zeros((rows_dense, LANES - routed - 2), bfloat)
    attention_pack = jnp.concatenate(
        [
            attention_in.astype(bfloat),
            attention_out.astype(bfloat),
            router.astype(bfloat),
            gains.T.astype(bfloat),
            pad_small,
        ],
        axis=1,
    )
    shared_pack = jnp.concatenate([shared_in, shared_out.T], axis=1).astype(bfloat)
    shared_pack = shared_pack.reshape(rows_dense, 3, narrow_count, quarter)
    shared_pack = jnp.pad(shared_pack, ((0, 0), (0, 0), (0, 0), (0, shared_width - quarter)))
    shared_pack = shared_pack.transpose(2, 0, 1, 3).reshape(
        narrow_count, rows_dense, 3 * shared_width
    )
    shared_piece = lax.all_to_all(
        shared_pack, "narrow", split_axis=0, concat_axis=0, tiled=True
    ).reshape(rows_plane, 3 * shared_width)
    expert_pack = jnp.concatenate(
        [experts_in, experts_out.transpose(0, 2, 1)], axis=2
    ).astype(bfloat)
    expert_piece = jnp.concatenate(
        [expert_pack[e] for e in range(EXP_DEV)] + [shared_piece], axis=1
    )

    route_hot = (routes[..., None] == jnp.arange(routed, dtype=jnp.int32)).astype(single).sum(axis=2)
    slot_hot_of_expert = (
        slot_order[:routed, None] == jnp.arange(slots, dtype=jnp.int32)
    ).astype(single)
    chosen = jnp.dot(route_hot.reshape(own_tokens, routed), slot_hot_of_expert)
    grad_out = cotangent.reshape(own_tokens, D)
    token_pack = jnp.concatenate(
        [grad_out, jnp.pad(chosen.astype(bfloat), ((0, 0), (0, LANES - slots)))], axis=1
    )
    token_parts = ring_gather(token_pack)

    attention_parts = ring_gather(attention_pack)
    attention_piece = place(attention_parts).reshape(rows_plane, ACOLS)
    attention_full = assemble(gather_plane(attention_piece))
    expert_full = assemble(gather_plane(expert_piece))

    w_attn_in = attention_full[:, : 3 * D]
    w_attn_out = attention_full[:, 3 * D : 4 * D]
    w_router = attention_full[:, 4 * D : 4 * D + routed]
    gain_rows = attention_full[:, 4 * D + routed : 4 * D + routed + 2].T.astype(single)
    router_slots = jnp.dot(w_router, slot_hot_of_expert.astype(bfloat))
    empty = jnp.sum(slot_hot_of_expert, axis=0) == 0.0

    rows_in = block_in.reshape(own_tokens, D).astype(single)
    grad_rows_out = grad_out.astype(single)
    positions = jnp.arange(MB_TOK, dtype=jnp.int32)
    scale_one = rms_scale(rows_in)
    first_norm = (rows_in * scale_one * gain_rows[0]).astype(bfloat)
    projected = dot(first_norm, w_attn_in).reshape(MB, MB_TOK, 3, HEADS, HEAD_DIM)
    cosines, sines = rotary_tables(positions - seq_ids)
    queries = rotate(projected[:, :, 0], cosines, sines).astype(bfloat)
    keys_rot = rotate(projected[:, :, 1], cosines, sines).astype(bfloat)
    values = projected[:, :, 2].astype(bfloat)
    allowed = (seq_ids[:, :, None] == seq_ids[:, None, :]) & (
        positions[None, None, :] <= positions[None, :, None]
    )
    scores = jnp.einsum(
        "bqhd,bkhd->bhqk", queries, keys_rot, preferred_element_type=single
    ) * HEAD_DIM ** (-0.5)
    scores = jnp.where(allowed[:, None], scores, MASKED)
    probs = jax.nn.softmax(scores, axis=-1)
    probs_low = probs.astype(bfloat)
    attended = (
        jnp.einsum("bhqk,bkhd->bqhd", probs_low, values, preferred_element_type=single)
        .astype(bfloat)
        .reshape(own_tokens, D)
    )
    hidden = rows_in + dot(attended, w_attn_out)
    scale_two = rms_scale(hidden)
    second_norm = (hidden * scale_two * gain_rows[1]).astype(bfloat)
    router_probs = jax.nn.softmax(
        jnp.where(empty, MASKED, dot(second_norm, router_slots)), axis=-1
    )

    norm_parts = ring_gather(second_norm)
    norm_all = jnp.concatenate(norm_parts, axis=0)
    token_all = jnp.concatenate(token_parts, axis=0)
    dy_all = token_all[:, :D]
    chosen_all = token_all[:, D : D + slots].astype(single)
    gates_all = chosen_all * jax.nn.softmax(
        jnp.where(empty, MASKED, dot(norm_all, router_slots)), axis=-1
    )
    chosen_mine = lax.dynamic_slice_in_dim(chosen_all, level * EXP_DEV, EXP_DEV, axis=1)
    gates_mine = lax.dynamic_slice_in_dim(gates_all, level * EXP_DEV, EXP_DEV, axis=1)
    chosen_mine = chosen_mine.reshape(blocks, MB_TOK, EXP_DEV)
    gates_mine = gates_mine.reshape(blocks, MB_TOK, EXP_DEV)
    below = (positions[:, None] > positions[None, :]).astype(single)
    ranks = jnp.einsum("tu,bue->bte", below, chosen_mine)
    select = (
        (ranks[:, :, :, None] == jnp.arange(capacity, dtype=single))
        & (chosen_mine[:, :, :, None] > 0.5)
    ).transpose(2, 0, 3, 1)
    select_low = select.astype(bfloat)
    count_rows = blocks * capacity
    norm_blocks = norm_all.reshape(blocks, MB_TOK, D)
    dy_blocks = dy_all.reshape(blocks, MB_TOK, D)

    out_sum = jnp.zeros((blocks, MB_TOK, D), single)
    grad_sum = jnp.zeros((blocks, MB_TOK, D), single)
    q_cols = []
    expert_grads = []
    for e in range(EXP_DEV):
        w_in = expert_full[:, e * ECOLS : e * ECOLS + 2 * FF]
        w_out = expert_full[:, e * ECOLS + 2 * FF : (e + 1) * ECOLS]
        sel = select_low[e]
        rows = jnp.einsum("brt,btd->brd", sel, norm_blocks, preferred_element_type=single)
        rows = rows.astype(bfloat).reshape(count_rows, D)
        dy_rows = jnp.einsum("brt,btd->brd", sel, dy_blocks, preferred_element_type=single)
        dy_rows = dy_rows.reshape(count_rows, D)
        gate_rows = jnp.sum(
            jnp.where(select[e], gates_mine[:, None, :, e], 0.0), axis=-1
        ).reshape(count_rows, 1)
        pre = dot(rows, w_in)
        gate_pre, up_pre = pre[:, :FF], pre[:, FF:]
        act = swiglu(gate_pre, up_pre).astype(bfloat)
        out = dot(act, w_out, NT).astype(bfloat).astype(single)
        q_rows = jnp.sum(out * dy_rows, axis=-1)
        q_cols.append(
            jnp.sum(
                jnp.where(select[e], q_rows.reshape(blocks, capacity, 1), 0.0), axis=1
            )
        )
        grad_rows_exp = (gate_rows * dy_rows).astype(bfloat)
        grad_act = dot(grad_rows_exp, w_out)
        grad_gate, grad_up = swiglu_back(gate_pre, up_pre, grad_act)
        grad_pre = jnp.concatenate([grad_gate, grad_up], axis=1).astype(bfloat)
        expert_grads.append(dot(rows, grad_pre, TN))
        expert_grads.append(dot(grad_rows_exp, act, TN))
        back = dot(grad_pre, w_in, NT).astype(bfloat).reshape(blocks, capacity, D)
        weighted = (gate_rows * out).astype(bfloat).reshape(blocks, capacity, D)
        out_sum += jnp.einsum("brt,brd->btd", sel, weighted, preferred_element_type=single)
        grad_sum += jnp.einsum("brt,brd->btd", sel, back, preferred_element_type=single)
    base = EXP_DEV * ECOLS
    w_gate = expert_full[:, base : base + shared_width]
    w_up = expert_full[:, base + shared_width : base + 2 * shared_width]
    w_down = expert_full[:, base + 2 * shared_width :]
    gate_pre, up_pre = dot(norm_all, w_gate), dot(norm_all, w_up)
    act = swiglu(gate_pre, up_pre).astype(bfloat)
    out_sum += dot(act, w_down, NT).reshape(blocks, MB_TOK, D)
    grad_gate, grad_up = swiglu_back(gate_pre, up_pre, dot(dy_all, w_down))
    grad_gate, grad_up = grad_gate.astype(bfloat), grad_up.astype(bfloat)
    grad_sum += (dot(grad_gate, w_gate, NT) + dot(grad_up, w_up, NT)).reshape(
        blocks, MB_TOK, D
    )
    expert_grads += [dot(norm_all, grad_gate, TN), dot(norm_all, grad_up, TN), dot(dy_all, act, TN)]
    expert_grads = [g.astype(bfloat) for g in expert_grads]

    out_parts = out_sum.reshape(narrow_count, own_tokens, D)
    grad_parts = grad_sum.reshape(narrow_count, own_tokens, D)
    q_sent = jnp.stack(q_cols, axis=-1).reshape(narrow_count, own_tokens, EXP_DEV)
    q_sent = place([q_sent[s] for s in range(narrow_count)])
    q_back = lax.all_to_all(q_sent, "narrow", split_axis=0, concat_axis=0, tiled=True)
    q_slots = q_back.transpose(1, 0, 2).reshape(own_tokens, slots)

    grad_second = ring_scatter(lambda s: grad_parts[s])
    grad_logits = router_probs * (
        q_slots - jnp.sum(router_probs * q_slots, axis=-1, keepdims=True)
    )
    grad_router = jnp.dot(
        jnp.dot(second_norm.astype(single).T, grad_logits, precision=HIGHEST),
        slot_hot_of_expert.T,
        precision=HIGHEST,
    )
    grad_second = grad_second + lax.dot_general(
        grad_logits, router_slots.astype(single), NT, precision=HIGHEST
    )
    grad_hidden_norm, grad_gain_two = norm_back(hidden, scale_two, gain_rows[1], grad_second)
    grad_hidden = grad_rows_out + grad_hidden_norm
    grad_branch = grad_hidden.astype(bfloat)
    grad_attn_out = dot(attended, grad_branch, TN)
    grad_attended = (
        dot(grad_branch, w_attn_out, NT).astype(bfloat).reshape(MB, MB_TOK, HEADS, HEAD_DIM)
    )
    grad_values = jnp.einsum(
        "bhqk,bqhd->bkhd", probs_low, grad_attended, preferred_element_type=single
    )
    grad_probs = jnp.einsum(
        "bqhd,bkhd->bhqk", grad_attended, values, preferred_element_type=single
    )
    grad_scores = (
        probs * (grad_probs - jnp.sum(probs * grad_probs, axis=-1, keepdims=True))
    ).astype(bfloat)
    grad_queries = jnp.einsum(
        "bhqk,bkhd->bqhd", grad_scores, keys_rot, preferred_element_type=single
    ) * HEAD_DIM ** (-0.5)
    grad_keys = jnp.einsum(
        "bhqk,bqhd->bkhd", grad_scores, queries, preferred_element_type=single
    ) * HEAD_DIM ** (-0.5)
    grad_projected = (
        jnp.stack(
            [rotate(grad_queries, cosines, -sines), rotate(grad_keys, cosines, -sines), grad_values],
            axis=2,
        )
        .astype(bfloat)
        .reshape(own_tokens, 3 * D)
    )
    grad_attn_in = dot(first_norm, grad_projected, TN)
    grad_first = dot(grad_projected, w_attn_in, NT)
    grad_rows_norm, grad_gain_one = norm_back(rows_in, scale_one, gain_rows[0], grad_first)
    input_grad = (grad_hidden + grad_rows_norm).astype(bfloat).reshape(MB, MB_TOK, D)

    routed_sum = ring_scatter(lambda s: out_parts[s])
    block_out = (hidden + routed_sum).astype(bfloat).reshape(MB, MB_TOK, D)

    attention_grads = jnp.concatenate(
        [
            grad_attn_in.astype(bfloat),
            grad_attn_out.astype(bfloat),
            grad_router.astype(bfloat),
            jnp.stack([grad_gain_one, grad_gain_two], axis=1).astype(bfloat),
            jnp.zeros((D, LANES - routed - 2), bfloat),
        ],
        axis=1,
    )
    expert_share = scatter_plane(jnp.concatenate(expert_grads, axis=1))
    attention_share = scatter_plane(attention_grads).reshape(narrow_count, rows_dense, ACOLS)
    attention_share = ring_scatter(
        lambda s: lax.dynamic_index_in_dim(
            attention_share, (level - s) % narrow_count, axis=0, keepdims=False
        )
    )
    shared_share = expert_share[:, base:].astype(bfloat).reshape(
        narrow_count, rows_dense, 3 * shared_width
    )
    shared_share = lax.all_to_all(
        shared_share, "narrow", split_axis=0, concat_axis=0, tiled=True
    ).reshape(narrow_count, rows_dense, 3, shared_width)[..., :quarter]
    shared_share = shared_share.transpose(1, 2, 0, 3).reshape(rows_dense, 3 * FF).astype(single)

    summed = (
        attention_share[:, : 3 * D],
        attention_share[:, 3 * D : 4 * D],
        shared_share[:, : 2 * FF],
        shared_share[:, 2 * FF :].T,
        attention_share[:, 4 * D : 4 * D + routed],
        attention_share[:, 4 * D + routed : 4 * D + routed + 2].T,
        jnp.stack([expert_share[:, e * ECOLS : e * ECOLS + 2 * FF] for e in range(EXP_DEV)]),
        jnp.stack(
            [expert_share[:, e * ECOLS + 2 * FF : (e + 1) * ECOLS].T for e in range(EXP_DEV)]
        ),
    )
    masters = (
        attention_in,
        attention_out,
        shared_in,
        shared_out,
        router,
        gains,
        experts_in,
        experts_out,
    )
    moments = (
        attention_in_moment,
        attention_out_moment,
        shared_in_moment,
        shared_out_moment,
        router_moment,
        gains_moment,
        experts_in_moment,
        experts_out_moment,
    )
    averages = (
        attention_in_average,
        attention_out_average,
        shared_in_average,
        shared_out_average,
        router_average,
        gains_average,
        experts_in_average,
        experts_out_average,
    )
    base_rate = 1.0 / math.sqrt(tokens)
    moment_outs = []
    states = []
    for master, moment, average, grad_share, step_rate in zip(
        masters, moments, averages, summed, STEP_RATES
    ):
        moment_new = MOMENTUM_DECAY * moment + grad_share
        master_new = master - step_rate * base_rate * (grad_share + MOMENTUM_DECAY * moment_new)
        average_new = AVERAGE_DECAY * average + (1.0 - AVERAGE_DECAY) * master_new
        moment_outs.append(moment_new)
        states.append(jnp.stack([average_new, master_new]))
    return (block_out, input_grad, *moment_outs, *states)


def solution(mesh):
    both = ("wide", "narrow")
    token = P(None, both, None)
    rows = P(both, None)
    cols = P(None, both)
    weight_specs = [rows, rows, rows, cols, rows, cols, P("narrow", "wide", None), P("narrow", None, "wide")]
    in_specs = (token, token, token, P(None, both), P()) + tuple(
        spec for spec in weight_specs for _ in range(3)
    )
    out_specs = (token, token, *weight_specs, *(P(None, *spec) for spec in weight_specs))
    return jax.shard_map(local, mesh=mesh, in_specs=in_specs, out_specs=out_specs, check_vma=False)
```

```python
import functools
import math

import jax
import jax.numpy as jnp
from jax import lax
from jax.experimental import pallas as pl
from jax.experimental.pallas import tpu as pltpu
from jax.sharding import PartitionSpec as P

D = 1280
HEADS = 10
HEAD_DIM = 128
FF = 896
TOPK = 7
EXP_DEV = 4
MB = 2
MB_TOK = 128
LANES = 128

EPSILON = 1e-06
MOMENTUM_DECAY = 0.9
AVERAGE_DECAY = 0.99
STEP_RATES = (0.006, 0.1, 0.009, 0.0125, 0.0002, 0.011, 0.027, 8.0)
MASKED = -1e30

ECOLS = 3 * FF
ACOLS = 4 * D + LANES
bfloat = jnp.bfloat16
single = jnp.float32


def split_cols(cols):
    return (cols // LANES + 1) // 2 * LANES


def dot(a, b, dims=(((1,), (0,)), ((), ()))):
    return lax.dot_general(a, b, dims, preferred_element_type=single)


NT = (((1,), (1,)), ((), ()))
TN = (((0,), (0,)), ((), ()))


def rms_scale(rows_in):
    return lax.rsqrt(jnp.mean(rows_in * rows_in, axis=-1, keepdims=True) + EPSILON)


def wide_xor(piece, bit):
    count = lax.axis_size("wide")
    return lax.ppermute(piece, "wide", [(i, i ^ bit) for i in range(count)])


def ring(piece):
    count = lax.axis_size("narrow")
    return lax.ppermute(piece, "narrow", [(i, (i + 1) % count) for i in range(count)])


def chip_bits():
    bits, bit = [], 2
    while bit < lax.axis_size("wide"):
        bits.append(bit)
        bit *= 2
    return bits


def gather_plane(left, right):
    halves = []
    for part, order in ((left, chip_bits()), (right, chip_bits()[::-1])):
        pieces = {0: part}
        for bit in order:
            pieces.update({r | bit: wide_xor(p, bit) for r, p in list(pieces.items())})
        pieces.update({r | 1: wide_xor(p, 1) for r, p in list(pieces.items())})
        halves.append([pieces[r] for r in range(lax.axis_size("wide"))])
    return halves


def place(pieces):
    level = lax.axis_index("narrow")
    count = len(pieces)
    full = jnp.zeros((count, *pieces[0].shape), pieces[0].dtype)
    for s, piece in enumerate(pieces):
        full = lax.dynamic_update_index_in_dim(full, piece, (level - s) % count, 0)
    return full


def scatter_half(keep, give, order):
    arrived = wide_xor(give, 1)
    terms = {i: [keep[i], arrived[i]] for i in range(keep.shape[0])}
    for bit in order:
        sent = [i for i in terms if i & (bit >> 1)]
        kept = [i for i in terms if not i & (bit >> 1)]
        outgoing = jnp.stack([sum(t.astype(single) for t in terms[i]).astype(bfloat) for i in sent])
        incoming = wide_xor(outgoing, bit)
        terms = {
            i: [*terms[i], incoming[sent.index(i | (bit >> 1))]]
            for i in kept
        }
    return sum(t.astype(single) for t in terms[0])


def scatter_plane(left, right):
    order = chip_bits()
    return (
        scatter_half(*left, order[::-1]),
        scatter_half(*right, order),
    )


TILE = 256


def col_tiles(width):
    return [(at, min(TILE, width - at)) for at in range(0, width, TILE)]


def expert_body(
    wide_count, narrow_count, capacity, width, first, buffers, idx, *refs
):
    refs = list(refs)
    take = lambda count: [refs.pop(0) for _ in range(count)]
    lefts, rights = take(wide_count), take(wide_count)
    norm_parts, dy_parts = take(narrow_count), take(narrow_count)
    rank_parts, gate_parts = take(narrow_count), take(narrow_count)
    sums_in = [] if first else take(2)
    keep_left, give_left, keep_right, give_right, q_ref = take(5)
    sums_out = take(2) if first else take(2 * narrow_count)
    (w, stage, norm, dy, out_acc, grad_acc, rows, dy_rows, grad_rows, pre, act, grad_pre, sel, sel_t, gate, q_acc, turned) = take(17)
    if width:
        sw, s_stage, s_act, s_pre = take(4)
    sems = refs.pop(0)
    assert not refs
    me, slot = idx[0], idx[1]
    part = norm_parts[0].shape[0]
    total = part * narrow_count
    shard = D // wide_count
    blocks = total // MB_TOK
    per_part = part // MB_TOK

    def row_of(r):
        return pl.multiple_of((me ^ r) * shard, 16)

    def slot_row(ref, number, at):
        tile = ref[:, at : at + MB_TOK]
        mine = lax.broadcasted_iota(jnp.int32, tile.shape, 0) == number
        return jnp.sum(jnp.where(mine, tile, 0.0), axis=0, keepdims=True)

    def weight_copies(halves, buffer, sem):
        return [
            pltpu.make_async_copy(
                halves[r].at[:, pl.ds(0, ECOLS)],
                w.at[buffer, pl.ds(row_of(r), shard), :],
                sems.at[sem],
            )
            for r in range(wide_count)
        ]

    token_copies = [
        pltpu.make_async_copy(src, dst.at[pl.ds(s * part, part), :], sems.at[2])
        for parts, dst in ((norm_parts, norm), (dy_parts, dy))
        for s, src in enumerate(parts)
    ]
    sum_copies = [
        pltpu.make_async_copy(src, dst, sems.at[3])
        for src, dst in zip(sums_in, (out_acc, grad_acc))
    ]
    shared_copies = []
    if width:
        for r in range(wide_count):
            shared_copies.append(
                pltpu.make_async_copy(
                    lefts[r].at[:, pl.ds(ECOLS, width)],
                    sw.at[pl.ds(row_of(r), shard), pl.ds(0, width)],
                    sems.at[4],
                )
            )
            shared_copies.append(
                pltpu.make_async_copy(
                    rights[r].at[:, pl.ds(ECOLS, 2 * width)],
                    sw.at[pl.ds(row_of(r), shard), pl.ds(width, 2 * width)],
                    sems.at[4],
                )
            )
    expert_copies = [weight_copies(lefts, 0, 0), weight_copies(rights, buffers - 1, 1)]
    for copy in token_copies + expert_copies[0] + sum_copies:
        copy.start()
    if buffers == 2:
        for copy in expert_copies[1]:
            copy.start()
    for copy in shared_copies:
        copy.start()
    for copy in token_copies:
        copy.wait()

    waiting = []
    for e in range(2):
        buffer = e if buffers == 2 else 0
        if e == 1 and buffers == 1:
            for copy in expert_copies[1]:
                copy.start()
        for b in range(blocks):
            s, at = b // per_part, (b % per_part) * MB_TOK
            rank_row = slot_row(rank_parts[s], slot + e, at)
            gate_row = slot_row(gate_parts[s], slot + e, at)
            place_in = lax.broadcasted_iota(jnp.int32, (capacity, MB_TOK), 0).astype(single)
            hit = jnp.where(place_in == rank_row, 1.0, 0.0)
            here = pl.ds(b * capacity, capacity)
            gate_col = jnp.sum(hit * gate_row, axis=1, keepdims=True)
            gate[here, :] = jnp.broadcast_to(gate_col, (capacity, LANES))
            hit_low = hit.astype(bfloat)
            sel[here, :] = hit_low
            sel_t[pl.ds(b * MB_TOK, MB_TOK), :] = hit.T.astype(bfloat)
            tokens_here = pl.ds(b * MB_TOK, MB_TOK)
            rows[here, :] = dot(hit_low, norm[tokens_here, :]).astype(bfloat)
            picked = dot(hit_low, dy[tokens_here, :])
            dy_rows[here, :] = picked.astype(bfloat)
            grad_rows[here, :] = (gate_col * picked).astype(bfloat)
        for copy in expert_copies[e]:
            copy.wait()

        @pl.loop(0, 2 * FF // TILE)
        def _(j):
            cols = pl.ds(pl.multiple_of(j * TILE, TILE), TILE)
            pre[:, cols] = dot(rows[...], w[buffer, :, cols])

        @pl.loop(0, rows.shape[0] // 32)
        def _(i):
            here = pl.ds(pl.multiple_of(i * 32, 32), 32)
            gate_pre, up_pre = pre[here, :FF], pre[here, FF:]
            sigma = jax.nn.sigmoid(gate_pre)
            silu = gate_pre * sigma
            act[here, :] = (silu * up_pre).astype(bfloat)
            pre[here, :FF] = up_pre * sigma * (1.0 + gate_pre * (1.0 - sigma))
            pre[here, FF:] = silu

        if e == 0:
            for copy in sum_copies:
                copy.wait()
        q_acc[...] = jnp.zeros_like(q_acc)

        def add_up(acc, tile, cols, fresh):
            for b in range(blocks):
                tokens_here = pl.ds(b * MB_TOK, MB_TOK)
                term = dot(sel_t[tokens_here, :], tile[b * capacity : (b + 1) * capacity, :])
                if fresh:
                    acc[tokens_here, cols] = term
                else:
                    acc[tokens_here, cols] += term

        @pl.loop(0, D // TILE)
        def _(j):
            cols = pl.ds(pl.multiple_of(j * TILE, TILE), TILE)
            out = dot(act[...], w[buffer, cols, 2 * FF :], NT).astype(bfloat).astype(single)
            product = out * dy_rows[:, cols].astype(single)
            q_acc[...] += product[:, :LANES] + product[:, LANES:]
            tile = (out * gate[:, :1]).astype(bfloat)
            add_up(out_acc, tile, cols, first and e == 0)

        q_col = jnp.sum(q_acc[...], axis=1, keepdims=True)
        for b in range(blocks):
            here = slice(b * capacity, (b + 1) * capacity)
            q_ref[e : e + 1, b * MB_TOK : (b + 1) * MB_TOK] = jnp.sum(
                sel[here, :].astype(single) * q_col[here], axis=0, keepdims=True
            )
        for at, n in col_tiles(FF):
            grad_act = dot(grad_rows[...], w[buffer, :, 2 * FF + at : 2 * FF + at + n])
            grad_pre[:, at : at + n] = (grad_act * pre[:, at : at + n]).astype(bfloat)
            grad_pre[:, FF + at : FF + at + n] = (
                grad_act * pre[:, FF + at : FF + at + n]
            ).astype(bfloat)

        @pl.loop(0, D // TILE)
        def _(j):
            cols = pl.ds(pl.multiple_of(j * TILE, TILE), TILE)
            tile = dot(grad_pre[...], w[buffer, cols, : 2 * FF], NT).astype(bfloat)
            add_up(grad_acc, tile, cols, first and e == 0)

        for copy in waiting:
            copy.wait()

        @pl.loop(0, D // TILE)
        def _(j):
            cols = pl.ds(pl.multiple_of(j * TILE, TILE), TILE)
            turned[...] = rows[:, cols].T

            @pl.loop(0, 2 * FF // TILE)
            def _(k):
                out_cols = pl.ds(pl.multiple_of(k * TILE, TILE), TILE)
                stage[cols, out_cols] = dot(turned[...], grad_pre[:, out_cols]).astype(bfloat)

            turned[...] = grad_rows[:, cols].T
            for at, n in col_tiles(FF):
                stage[cols, 2 * FF + at : 2 * FF + at + n] = dot(
                    turned[...], act[:, at : at + n]
                ).astype(bfloat)

        keep, give = ((keep_left, give_left), (keep_right, give_right))[e]
        waiting = [
            pltpu.make_async_copy(
                stage.at[pl.ds(row_of(r), shard), :],
                (give if r & 1 else keep).at[r // 2, :, pl.ds(0, ECOLS)],
                sems.at[5],
            )
            for r in range(wide_count)
        ]
        for copy in waiting:
            copy.start()

    if width:
        for copy in shared_copies:
            copy.wait()

        @pl.loop(0, total // TILE)
        def _(i):
            here = pl.ds(pl.multiple_of(i * TILE, TILE), TILE)
            gate_pre = dot(norm[here, :], sw[:, :width])
            up_pre = dot(norm[here, :], sw[:, width : 2 * width])
            sigma = jax.nn.sigmoid(gate_pre)
            silu = gate_pre * sigma
            s_act[here, :] = (silu * up_pre).astype(bfloat)
            grad_act = dot(dy[here, :], sw[:, 2 * width :])
            s_pre[here, :width] = (
                grad_act * up_pre * sigma * (1.0 + gate_pre * (1.0 - sigma))
            ).astype(bfloat)
            s_pre[here, width:] = (grad_act * silu).astype(bfloat)
            for at, n in col_tiles(D):
                cols = slice(at, at + n)
                out_acc[here, cols] += dot(s_act[here, :], sw[cols, 2 * width :], NT)
                grad_acc[here, cols] += dot(s_pre[here, :], sw[cols, : 2 * width], NT)

        @pl.loop(0, D // TILE)
        def _(j):
            cols = pl.ds(pl.multiple_of(j * TILE, TILE), TILE)
            s_stage[cols, : 2 * width] = dot(norm[:, cols], s_pre[...], TN).astype(bfloat)
            s_stage[cols, 2 * width :] = dot(dy[:, cols], s_act[...], TN).astype(bfloat)

        for r in range(wide_count):
            for ref_pair, at, n in (
                ((keep_left, give_left), 0, width),
                ((keep_right, give_right), width, 2 * width),
            ):
                copy = pltpu.make_async_copy(
                    s_stage.at[pl.ds(row_of(r), shard), pl.ds(at, n)],
                    ref_pair[r & 1].at[r // 2, :, pl.ds(ECOLS, n)],
                    sems.at[6],
                )
                copy.start()
                waiting.append(copy)
    if first:
        finals = [
            pltpu.make_async_copy(src, dst, sems.at[7])
            for src, dst in zip((out_acc, grad_acc), sums_out)
        ]
        for copy in finals:
            copy.start()
    else:
        finals = []
        for acc, low, outs in (
            (out_acc, norm, sums_out[:narrow_count]),
            (grad_acc, dy, sums_out[narrow_count:]),
        ):
            finals.append(pltpu.make_async_copy(acc.at[pl.ds(0, part), :], outs[0], sems.at[7]))
            finals[-1].start()
            for s in range(1, narrow_count):

                @pl.loop(0, part // 32)
                def _(i):
                    here = pl.ds(pl.multiple_of(s * part + i * 32, 32), 32)
                    low[here, :] = acc[here, :].astype(bfloat)

                finals.append(
                    pltpu.make_async_copy(low.at[pl.ds(s * part, part), :], outs[s], sems.at[7])
                )
                finals[-1].start()
    for copy in waiting + finals:
        copy.wait()


def expert_pair(lefts, rights, norm_parts, dy_parts, rank_parts, gate_parts, sums, index, capacity, width):
    wide_count, narrow_count = len(lefts), len(norm_parts)
    shard = D // wide_count
    part = norm_parts[0].shape[0]
    total = part * narrow_count
    count_rows = total // MB_TOK * capacity
    first = sums is None
    buffers = 2 if narrow_count <= 4 else 1
    left_cols, right_cols = lefts[0].shape[1], rights[0].shape[1]
    grads = lambda cols: jax.ShapeDtypeStruct((wide_count // 2, shard, cols), bfloat)
    if first:
        sum_shapes = [jax.ShapeDtypeStruct((total, D), single)] * 2
    else:
        sum_shapes = (
            [jax.ShapeDtypeStruct((part, D), single)]
            + [jax.ShapeDtypeStruct((part, D), bfloat)] * (narrow_count - 1)
        ) * 2
    any_space = pl.BlockSpec(memory_space=pl.ANY)
    vmem = pl.BlockSpec(memory_space=pltpu.VMEM)
    operands = [*lefts, *rights, *norm_parts, *dy_parts, *rank_parts, *gate_parts]
    specs = [any_space] * (2 * wide_count + 2 * narrow_count) + [vmem] * (2 * narrow_count)
    if not first:
        operands += list(sums)
        specs += [any_space] * 2
    scratch = [
        pltpu.VMEM((buffers, D, ECOLS), bfloat),
        pltpu.VMEM((D, ECOLS), bfloat),
        pltpu.VMEM((total, D), bfloat),
        pltpu.VMEM((total, D), bfloat),
        pltpu.VMEM((total, D), single),
        pltpu.VMEM((total, D), single),
        pltpu.VMEM((count_rows, D), bfloat),
        pltpu.VMEM((count_rows, D), bfloat),
        pltpu.VMEM((count_rows, D), bfloat),
        pltpu.VMEM((count_rows, 2 * FF), single),
        pltpu.VMEM((count_rows, FF), bfloat),
        pltpu.VMEM((count_rows, 2 * FF), bfloat),
        pltpu.VMEM((count_rows, MB_TOK), bfloat),
        pltpu.VMEM((total, capacity), bfloat),
        pltpu.VMEM((count_rows, LANES), single),
        pltpu.VMEM((count_rows, LANES), single),
        pltpu.VMEM((TILE, count_rows), bfloat),
    ]
    if width:
        scratch += [
            pltpu.VMEM((D, 3 * width), bfloat),
            pltpu.VMEM((D, 3 * width), bfloat),
            pltpu.VMEM((total, width), bfloat),
            pltpu.VMEM((total, 2 * width), bfloat),
        ]
    scratch.append(pltpu.SemaphoreType.DMA((8,)))
    flops = 2 * 2 * count_rows * 9 * D * FF + 6 * 2 * total * D * width
    results = pl.pallas_call(
        functools.partial(
            expert_body, wide_count, narrow_count, capacity, width, first, buffers
        ),
        out_shape=[
            grads(left_cols),
            grads(left_cols),
            grads(right_cols),
            grads(right_cols),
            jax.ShapeDtypeStruct((2, total), single),
            *sum_shapes,
        ],
        in_specs=[pl.BlockSpec(memory_space=pltpu.SMEM)] + specs,
        out_specs=[any_space] * 4 + [vmem] + [any_space] * len(sum_shapes),
        scratch_shapes=scratch,
        compiler_params=pltpu.CompilerParams(vmem_limit_bytes=60 * 2**20),
        cost_estimate=pl.CostEstimate(
            flops=flops, bytes_accessed=4 * D * (left_cols + right_cols), transcendentals=0
        ),
    )(index, *operands)
    return results[:4], results[4], results[5:]


def ring_gather(piece):
    pieces = [piece]
    for _ in range(lax.axis_size("narrow") - 1):
        pieces.append(ring(pieces[-1]))
    return pieces


def ring_scatter(parts):
    count = lax.axis_size("narrow")
    total = parts[1].astype(bfloat)
    for step in range(2, count):
        total = (ring(total).astype(single) + parts[step].astype(single)).astype(bfloat)
    return parts[0], ring(total)


def pack_copies(w, lefts, rights, me, sem):
    shard = lefts[0].shape[0]
    cut = lefts[0].shape[1]
    copies = []
    for r, (left, right) in enumerate(zip(lefts, rights)):
        here = pl.ds(pl.multiple_of((me ^ r) * shard, 16), shard)
        copies.append(pltpu.make_async_copy(left, w.at[here, pl.ds(0, cut)], sem))
        copies.append(pltpu.make_async_copy(right, w.at[here, pl.ds(cut, ACOLS - cut)], sem))
    return copies


def turn(vectors, cosines, sines):
    return vectors * cosines + pltpu.roll(vectors, HEAD_DIM // 2, 1) * sines


def head_cols(part, head):
    return pl.ds(pl.multiple_of(part * D + head * HEAD_DIM, LANES), HEAD_DIM)


def row_probs(queries, keys_rot, bias):
    scores = dot(queries, keys_rot, NT) * HEAD_DIM ** (-0.5) + bias
    exp_scores = jnp.exp(scores - jnp.max(scores, axis=-1, keepdims=True))
    return exp_scores / jnp.sum(exp_scores, axis=-1, keepdims=True)


def attention_forward_body(wide_count, routed, idx, *refs):
    refs = list(refs)
    take = lambda count: [refs.pop(0) for _ in range(count)]
    lefts, rights = take(wide_count), take(wide_count)
    x, cosines, sines, bias, perm, slot_bias = take(6)
    hidden, second_norm, first_norm, qkv, attended, router_probs, gates, gain_rows = take(8)
    w, projected, sem = refs
    copies = pack_copies(w, lefts, rights, idx[0], sem)
    for copy in copies:
        copy.start()
    for copy in copies:
        copy.wait()
    tail = w[:, 4 * D :]
    gain_rows[...] = tail.astype(single).T[routed : routed + 2, :]
    rows_in = x[...].astype(single)
    first_norm[...] = (rows_in * rms_scale(rows_in) * gain_rows[0:1, :]).astype(bfloat)

    @pl.loop(0, 3 * D // TILE)
    def _(j):
        cols = pl.ds(pl.multiple_of(j * TILE, TILE), TILE)
        projected[:, cols] = dot(first_norm[...], w[:, cols])

    @pl.loop(0, HEADS)
    def _(head):
        for part in range(2):
            cols = head_cols(part, head)
            qkv[:, cols] = turn(projected[:, cols], cosines[...], sines[...]).astype(bfloat)
        cols = head_cols(2, head)
        qkv[:, cols] = projected[:, cols].astype(bfloat)
        for b in range(MB):
            here = slice(b * MB_TOK, (b + 1) * MB_TOK)
            probs = row_probs(
                qkv[here, head_cols(0, head)], qkv[here, head_cols(1, head)], bias[here, :]
            ).astype(bfloat)
            attended[here, head_cols(0, head)] = dot(probs, qkv[here, cols]).astype(bfloat)

    for at, n in col_tiles(D):
        hidden[:, at : at + n] = rows_in[:, at : at + n] + dot(
            attended[...], w[:, 3 * D + at : 3 * D + at + n]
        )
    rows_mid = hidden[...]
    second_norm[...] = (rows_mid * rms_scale(rows_mid) * gain_rows[1:2, :]).astype(bfloat)
    router_slots = dot(tail, perm[...]).astype(bfloat)
    logits = dot(second_norm[...], router_slots) + slot_bias[...]
    exp_logits = jnp.exp(logits - jnp.max(logits, axis=-1, keepdims=True))
    probs = exp_logits / jnp.sum(exp_logits, axis=-1, keepdims=True)
    router_probs[...] = probs
    gates[...] = probs.T[: gates.shape[0], :]


def attention_backward_body(wide_count, routed, slots, idx, *refs):
    refs = list(refs)
    take = lambda count: [refs.pop(0) for _ in range(count)]
    lefts, rights = take(wide_count), take(wide_count)
    x, cosines, sines, bias, perm = take(5)
    hidden, second_norm, first_norm, qkv, attended, router_probs, gain_rows = take(7)
    dy, second_own, second_come, q_rows = take(4)
    keep_left, give_left, keep_right, give_right, input_grad = take(5)
    w, stage, grad_second, grad_hidden, grad_branch, grad_attended, grad_projected, turned, tail_rows, sems = refs
    me = idx[0]
    copies = pack_copies(w, lefts, rights, me, sems.at[0])
    for copy in copies:
        copy.start()
    for copy in copies:
        copy.wait()
    probs = router_probs[...]
    pad = jnp.zeros((LANES - slots, q_rows.shape[1]), single)
    q = jnp.concatenate([q_rows[...], pad], axis=0).T
    grad_logits = probs * (q - jnp.sum(probs * q, axis=-1, keepdims=True))
    high = grad_logits.astype(bfloat)
    rest = (grad_logits - high.astype(single)).astype(bfloat)
    router_slots = dot(w[:, 4 * D :], perm[...]).astype(bfloat)
    for at, n in col_tiles(D):
        cols = slice(at, at + n)
        grad_second[:, cols] = (
            second_own[:, cols]
            + second_come[:, cols].astype(single)
            + dot(high, router_slots[cols, :], NT)
            + dot(rest, router_slots[cols, :], NT)
        )
    tail_rows[...] = jnp.zeros_like(tail_rows)
    rows_mid = hidden[...]
    scale = rms_scale(rows_mid)
    normed = rows_mid * scale
    weighted = grad_second[...] * gain_rows[1:2, :]
    tail_rows[1:2, :] = jnp.sum(grad_second[...] * normed, axis=0, keepdims=True)
    grad_hidden[...] = dy[...].astype(single) + scale * (
        weighted - normed * jnp.mean(weighted * normed, axis=-1, keepdims=True)
    )
    grad_branch[...] = grad_hidden[...].astype(bfloat)

    @pl.loop(0, D // TILE)
    def _(j):
        cols = pl.ds(pl.multiple_of(j * TILE, TILE), TILE)
        grad_attended[:, cols] = dot(grad_branch[...], w[cols, 3 * D : 4 * D], NT).astype(bfloat)
        turned[...] = attended[:, cols].T

        for at, n in col_tiles(D):
            stage[cols, 3 * D + at : 3 * D + at + n] = dot(
                turned[...], grad_branch[:, at : at + n]
            ).astype(bfloat)

    @pl.loop(0, HEADS)
    def _(head):
        for b in range(MB):
            here = slice(b * MB_TOK, (b + 1) * MB_TOK)
            queries = qkv[here, head_cols(0, head)]
            keys_rot = qkv[here, head_cols(1, head)]
            values = qkv[here, head_cols(2, head)]
            probs = row_probs(queries, keys_rot, bias[here, :])
            grad_out = grad_attended[here, head_cols(0, head)]
            grad_values = dot(probs.astype(bfloat), grad_out, TN)
            grad_probs = dot(grad_out, values, NT)
            grad_scores = probs * (
                grad_probs - jnp.sum(probs * grad_probs, axis=-1, keepdims=True)
            )
            grad_scores = grad_scores.astype(bfloat)
            grad_queries = dot(grad_scores, keys_rot) * HEAD_DIM ** (-0.5)
            grad_keys = dot(grad_scores, queries, TN) * HEAD_DIM ** (-0.5)
            for part, grad in enumerate((grad_queries, grad_keys)):
                grad_projected[here, head_cols(part, head)] = turn(
                    grad, cosines[here, :], -sines[here, :]
                ).astype(bfloat)
            grad_projected[here, head_cols(2, head)] = grad_values.astype(bfloat)

    @pl.loop(0, D // TILE)
    def _(j):
        cols = pl.ds(pl.multiple_of(j * TILE, TILE), TILE)
        grad_second[:, cols] = dot(grad_projected[...], w[cols, : 3 * D], NT)
        turned[...] = first_norm[:, cols].T

        @pl.loop(0, 3 * D // TILE)
        def _(k):
            out_cols = pl.ds(pl.multiple_of(k * TILE, TILE), TILE)
            stage[cols, out_cols] = dot(turned[...], grad_projected[:, out_cols]).astype(bfloat)

    rows_in = x[...].astype(single)
    scale = rms_scale(rows_in)
    normed = rows_in * scale
    weighted = grad_second[...] * gain_rows[0:1, :]
    tail_rows[0:1, :] = jnp.sum(grad_second[...] * normed, axis=0, keepdims=True)
    input_grad[...] = (
        grad_hidden[...]
        + scale * (weighted - normed * jnp.mean(weighted * normed, axis=-1, keepdims=True))
    ).astype(bfloat)
    high_expert = dot(high, perm[...], NT).astype(bfloat)
    rest_expert = dot(rest, perm[...], NT).astype(bfloat)
    lane = lax.broadcasted_iota(jnp.int32, (TILE, LANES), 1)
    for at, n in col_tiles(D):
        gain_cols = tail_rows[:, at : at + n].T
        router_cols = dot(second_norm[:, at : at + n], high_expert, TN) + dot(
            second_norm[:, at : at + n], rest_expert, TN
        )
        stage[at : at + n, 4 * D :] = (
            router_cols
            + jnp.where(lane == routed, gain_cols[:, 0:1], 0.0)
            + jnp.where(lane == routed + 1, gain_cols[:, 1:2], 0.0)
        ).astype(bfloat)
    shard = D // wide_count
    cut = split_cols(ACOLS)
    copies = []
    for r in range(wide_count):
        here = pl.ds(pl.multiple_of((me ^ r) * shard, 16), shard)
        for refs_out, at, n in (
            ((keep_left, give_left), 0, cut),
            ((keep_right, give_right), cut, ACOLS - cut),
        ):
            copies.append(
                pltpu.make_async_copy(
                    stage.at[here, pl.ds(at, n)], refs_out[r & 1].at[r // 2], sems.at[1]
                )
            )
    for copy in copies:
        copy.start()
    for copy in copies:
        copy.wait()


def attention_forward(lefts, rights, operands, index, routed, slots):
    wide_count = len(lefts)
    part = operands[0].shape[0]
    out = jax.ShapeDtypeStruct
    vmem = pl.BlockSpec(memory_space=pltpu.VMEM)
    any_space = pl.BlockSpec(memory_space=pl.ANY)
    return pl.pallas_call(
        functools.partial(attention_forward_body, wide_count, routed),
        out_shape=[
            out((part, D), single),
            out((part, D), bfloat),
            out((part, D), bfloat),
            out((part, 3 * D), bfloat),
            out((part, D), bfloat),
            out((part, LANES), single),
            out((slots, part), single),
            out((2, D), single),
        ],
        in_specs=[pl.BlockSpec(memory_space=pltpu.SMEM)]
        + [any_space] * (2 * wide_count)
        + [vmem] * len(operands),
        out_specs=[vmem] * 8,
        scratch_shapes=[
            pltpu.VMEM((D, ACOLS), bfloat),
            pltpu.VMEM((part, 3 * D), single),
            pltpu.SemaphoreType.DMA,
        ],
        compiler_params=pltpu.CompilerParams(vmem_limit_bytes=60 * 2**20),
        cost_estimate=pl.CostEstimate(
            flops=8 * part * D * D, bytes_accessed=2 * D * ACOLS, transcendentals=0
        ),
    )(index, *lefts, *rights, *operands)


def attention_backward(lefts, rights, operands, index, routed, slots):
    wide_count = len(lefts)
    part = operands[0].shape[0]
    out = jax.ShapeDtypeStruct
    vmem = pl.BlockSpec(memory_space=pltpu.VMEM)
    any_space = pl.BlockSpec(memory_space=pl.ANY)
    cut = split_cols(ACOLS)
    shard = D // wide_count
    grads = lambda cols: out((wide_count // 2, shard, cols), bfloat)
    return pl.pallas_call(
        functools.partial(attention_backward_body, wide_count, routed, slots),
        out_shape=[
            grads(cut),
            grads(cut),
            grads(ACOLS - cut),
            grads(ACOLS - cut),
            out((part, D), bfloat),
        ],
        in_specs=[pl.BlockSpec(memory_space=pltpu.SMEM)]
        + [any_space] * (2 * wide_count)
        + [vmem] * len(operands),
        out_specs=[any_space] * 4 + [vmem],
        scratch_shapes=[
            pltpu.VMEM((D, ACOLS), bfloat),
            pltpu.VMEM((D, ACOLS), bfloat),
            pltpu.VMEM((part, D), single),
            pltpu.VMEM((part, D), single),
            pltpu.VMEM((part, D), bfloat),
            pltpu.VMEM((part, D), bfloat),
            pltpu.VMEM((part, 3 * D), bfloat),
            pltpu.VMEM((TILE, part), bfloat),
            pltpu.VMEM((8, D), single),
            pltpu.SemaphoreType.DMA((2,)),
        ],
        compiler_params=pltpu.CompilerParams(vmem_limit_bytes=60 * 2**20),
        cost_estimate=pl.CostEstimate(
            flops=16 * part * D * D, bytes_accessed=6 * D * ACOLS, transcendentals=0
        ),
    )(index, *lefts, *rights, *operands)


def local(
    block_in,
    cotangent,
    routes,
    seq_ids,
    slot_order,
    attention_in,
    attention_in_moment,
    attention_in_average,
    attention_out,
    attention_out_moment,
    attention_out_average,
    shared_in,
    shared_in_moment,
    shared_in_average,
    shared_out,
    shared_out_moment,
    shared_out_average,
    router,
    router_moment,
    router_average,
    gains,
    gains_moment,
    gains_average,
    experts_in,
    experts_in_moment,
    experts_in_average,
    experts_out,
    experts_out_moment,
    experts_out_average,
):
    wide_count = lax.axis_size("wide")
    narrow_count = lax.axis_size("narrow")
    level = lax.axis_index("narrow")
    slots = EXP_DEV * narrow_count
    routed = slots - 1
    capacity = (MB_TOK * TOPK * 8 // (7 * slots) + 7) // 8 * 8
    tokens = MB * MB_TOK * wide_count * narrow_count
    own_tokens = MB * MB_TOK
    rows_dense = D // (wide_count * narrow_count)
    rows_plane = D // wide_count
    quarter = FF // narrow_count
    shared_width = (quarter + LANES - 1) // LANES * LANES

    pad_small = jnp.zeros((rows_dense, LANES - routed - 2), bfloat)
    attention_pack = jnp.concatenate(
        [
            attention_in.astype(bfloat),
            attention_out.astype(bfloat),
            router.astype(bfloat),
            gains.T.astype(bfloat),
            pad_small,
        ],
        axis=1,
    )
    shared_pack = jnp.concatenate([shared_in, shared_out.T], axis=1).astype(bfloat)
    shared_pack = shared_pack.reshape(rows_dense, 3, narrow_count, quarter)
    shared_pack = jnp.pad(shared_pack, ((0, 0), (0, 0), (0, 0), (0, shared_width - quarter)))
    shared_pack = shared_pack.transpose(2, 0, 1, 3).reshape(
        narrow_count, rows_dense, 3 * shared_width
    )
    shared_piece = lax.all_to_all(
        shared_pack, "narrow", split_axis=0, concat_axis=0, tiled=True
    ).reshape(rows_plane, 3 * shared_width)
    expert_pack = jnp.concatenate(
        [experts_in, experts_out.transpose(0, 2, 1)], axis=2
    ).astype(bfloat)
    expert_halves = [
        (expert_pack[0], expert_pack[1]),
        (
            jnp.concatenate([expert_pack[2], shared_piece[:, :shared_width]], axis=1),
            jnp.concatenate([expert_pack[3], shared_piece[:, shared_width:]], axis=1),
        ),
    ]

    route_hot = (routes[..., None] == jnp.arange(routed, dtype=jnp.int32)).astype(single).sum(axis=2)
    slot_hot_of_expert = (
        slot_order[:routed, None] == jnp.arange(slots, dtype=jnp.int32)
    ).astype(single)
    chosen = jnp.dot(route_hot.reshape(own_tokens, routed), slot_hot_of_expert)
    positions = jnp.arange(MB_TOK, dtype=jnp.int32)
    below = (positions[:, None] > positions[None, :]).astype(bfloat)
    ranks = jnp.einsum(
        "tu,bue->bte", below, chosen.reshape(MB, MB_TOK, slots).astype(bfloat), preferred_element_type=single
    ).reshape(own_tokens, slots)
    rank_parts = ring_gather(jnp.where(chosen > 0.5, ranks, -1.0).T)
    grad_out = cotangent.reshape(own_tokens, D)
    dy_parts = ring_gather(grad_out)

    attention_parts = ring_gather(attention_pack)
    attention_piece = place(attention_parts).reshape(rows_plane, ACOLS)
    cut = split_cols(ACOLS)
    attention_halves = gather_plane(attention_piece[:, :cut], attention_piece[:, cut:])
    expert_full = [gather_plane(*halves) for halves in expert_halves]

    wide_index = lax.axis_index("wide").reshape(1)
    perm = jnp.pad(
        slot_hot_of_expert, ((0, LANES - routed), (0, LANES - slots))
    ).astype(bfloat)
    slot_bias = jnp.where(jnp.sum(perm.astype(single), axis=0, keepdims=True) > 0.0, 0.0, MASKED)
    half_dim = HEAD_DIM // 2
    freqs = jnp.exp(jnp.arange(half_dim, dtype=single) * (-2.0 * math.log(10000.0) / HEAD_DIM))
    angles = (positions - seq_ids).reshape(own_tokens, 1).astype(single) * freqs
    cosines, sines = jnp.cos(angles), jnp.sin(angles)
    cosines = jnp.concatenate([cosines, cosines], axis=1)
    sines = jnp.concatenate([-sines, sines], axis=1)
    allowed = (seq_ids[:, :, None] == seq_ids[:, None, :]) & (
        positions[None, None, :] <= positions[None, :, None]
    )
    bias = jnp.where(allowed, 0.0, MASKED).reshape(own_tokens, MB_TOK)
    rows_in = block_in.reshape(own_tokens, D)
    tables = (cosines, sines, bias, perm)
    hidden, second_norm, first_norm, qkv, attended, router_probs, gates, gain_rows = attention_forward(
        *attention_halves, (rows_in, *tables, slot_bias), wide_index, routed, slots
    )

    norm_parts = ring_gather(second_norm)
    gate_parts = ring_gather(gates)
    sums = None
    expert_grads, q_rows = [], []
    for pair in range(2):
        index = jnp.stack([lax.axis_index("wide"), level * EXP_DEV + 2 * pair])
        grads, q_pair, sums = expert_pair(
            *expert_full[pair],
            norm_parts,
            dy_parts,
            rank_parts,
            gate_parts,
            sums,
            index,
            capacity,
            shared_width if pair else 0,
        )
        expert_grads.append(grads)
        q_rows.append(q_pair)
    out_parts, grad_parts = sums[:narrow_count], sums[narrow_count:]
    q_sent = jnp.concatenate(q_rows, axis=0).reshape(EXP_DEV, narrow_count, own_tokens)
    q_sent = place([q_sent[:, s] for s in range(narrow_count)])
    q_back = lax.all_to_all(q_sent, "narrow", split_axis=0, concat_axis=0, tiled=True)
    q_back = q_back.reshape(slots, own_tokens)
    second_own, second_come = ring_scatter(grad_parts)
    *attention_grads, input_grad = attention_backward(
        *attention_halves,
        (
            rows_in,
            *tables,
            hidden,
            second_norm,
            first_norm,
            qkv,
            attended,
            router_probs,
            gain_rows,
            grad_out,
            second_own,
            second_come,
            q_back,
        ),
        wide_index,
        routed,
        slots,
    )
    input_grad = input_grad.reshape(MB, MB_TOK, D)

    out_own, out_come = ring_scatter(out_parts)
    block_out = hidden + out_own + out_come.astype(single)
    block_out = block_out.astype(bfloat).reshape(MB, MB_TOK, D)

    shares = [scatter_plane(grads[:2], grads[2:]) for grads in expert_grads]
    attention_share = jnp.concatenate(
        scatter_plane(attention_grads[:2], attention_grads[2:]),
        axis=1,
    ).reshape(narrow_count, rows_dense, ACOLS)
    attention_own, attention_come = ring_scatter(
        [
            lax.dynamic_index_in_dim(attention_share, (level - s) % narrow_count, 0, False)
            for s in range(narrow_count)
        ]
    )
    attention_share = attention_own + attention_come.astype(single)
    shared_share = (
        jnp.concatenate([shares[1][0][:, ECOLS:], shares[1][1][:, ECOLS:]], axis=1)
        .astype(bfloat)
        .reshape(narrow_count, rows_dense, 3 * shared_width)
    )
    expert_shares = [half[:, :ECOLS] for pair in shares for half in pair]
    shared_share = lax.all_to_all(
        shared_share, "narrow", split_axis=0, concat_axis=0, tiled=True
    ).reshape(narrow_count, rows_dense, 3, shared_width)[..., :quarter]
    shared_share = shared_share.transpose(1, 2, 0, 3).reshape(rows_dense, 3 * FF).astype(single)

    summed = (
        attention_share[:, : 3 * D],
        attention_share[:, 3 * D : 4 * D],
        shared_share[:, : 2 * FF],
        shared_share[:, 2 * FF :].T,
        attention_share[:, 4 * D : 4 * D + routed],
        attention_share[:, 4 * D + routed : 4 * D + routed + 2].T,
        jnp.stack([share[:, : 2 * FF] for share in expert_shares]),
        jnp.stack([share[:, 2 * FF :].T for share in expert_shares]),
    )
    masters = (
        attention_in,
        attention_out,
        shared_in,
        shared_out,
        router,
        gains,
        experts_in,
        experts_out,
    )
    moments = (
        attention_in_moment,
        attention_out_moment,
        shared_in_moment,
        shared_out_moment,
        router_moment,
        gains_moment,
        experts_in_moment,
        experts_out_moment,
    )
    averages = (
        attention_in_average,
        attention_out_average,
        shared_in_average,
        shared_out_average,
        router_average,
        gains_average,
        experts_in_average,
        experts_out_average,
    )
    base_rate = 1.0 / math.sqrt(tokens)
    moment_outs = []
    states = []
    for master, moment, average, grad_share, step_rate in zip(
        masters, moments, averages, summed, STEP_RATES
    ):
        moment_new = MOMENTUM_DECAY * moment + grad_share
        master_new = master - step_rate * base_rate * (grad_share + MOMENTUM_DECAY * moment_new)
        average_new = AVERAGE_DECAY * average + (1.0 - AVERAGE_DECAY) * master_new
        moment_outs.append(moment_new)
        states.append(jnp.stack([average_new, master_new]))
    return (block_out, input_grad, *moment_outs, *states)


def solution(mesh):
    both = ("wide", "narrow")
    token = P(None, both, None)
    rows = P(both, None)
    cols = P(None, both)
    weight_specs = [rows, rows, rows, cols, rows, cols, P("narrow", "wide", None), P("narrow", None, "wide")]
    in_specs = (token, token, token, P(None, both), P()) + tuple(
        spec for spec in weight_specs for _ in range(3)
    )
    out_specs = (token, token, *weight_specs, *(P(None, *spec) for spec in weight_specs))
    return jax.shard_map(local, mesh=mesh, in_specs=in_specs, out_specs=out_specs, check_vma=False)
```

```python
import functools
import math

import jax
import jax.numpy as jnp
from jax import lax
from jax.experimental import pallas as pl
from jax.experimental.pallas import tpu as pltpu
from jax.sharding import PartitionSpec as P

D = 1280
HEADS = 10
HEAD_DIM = 128
FF = 896
TOPK = 7
EXP_DEV = 4
MB = 2
MB_TOK = 128
LANES = 128

EPSILON = 1e-06
MOMENTUM_DECAY = 0.9
AVERAGE_DECAY = 0.99
STEP_RATES = (0.006, 0.1, 0.009, 0.0125, 0.0002, 0.011, 0.027, 8.0)
MASKED = -1e30

ECOLS = 3 * FF
ACOLS = 4 * D + LANES
bfloat = jnp.bfloat16
single = jnp.float32


def split_cols(cols):
    return (cols // LANES + 1) // 2 * LANES


def dot(a, b, dims=(((1,), (0,)), ((), ()))):
    return lax.dot_general(a, b, dims, preferred_element_type=single)


NT = (((1,), (1,)), ((), ()))
TN = (((0,), (0,)), ((), ()))


def rms_scale(rows_in):
    return lax.rsqrt(jnp.mean(rows_in * rows_in, axis=-1, keepdims=True) + EPSILON)


def wide_xor(piece, bit):
    count = lax.axis_size("wide")
    return lax.ppermute(piece, "wide", [(i, i ^ bit) for i in range(count)])


def ring(piece):
    count = lax.axis_size("narrow")
    return lax.ppermute(piece, "narrow", [(i, (i + 1) % count) for i in range(count)])


def chip_bits():
    bits, bit = [], 2
    while bit < lax.axis_size("wide"):
        bits.append(bit)
        bit *= 2
    return bits


def after(value, *others):
    return lax.optimization_barrier((value, *others))[0]


def first_hops(pieces, bit):
    return {r | bit: wide_xor(p, bit) for r, p in pieces.items()}


def core_hops(pieces, pairs=False):
    full = {r: (p, wide_xor(p, 1)) for r, p in pieces.items()}
    return full if pairs else [p for r in sorted(full) for p in full[r]]


def gather_chips(piece, order, held=None, wait=()):
    pieces = {0: piece}
    for number, bit in enumerate(order):
        if number == 0 and held is not None:
            pieces.update(held)
            continue
        source = dict(pieces)
        if wait:
            source = {r: after(p, *wait) for r, p in source.items()}
        pieces.update(first_hops(source, bit))
    return pieces


def place(pieces):
    level = lax.axis_index("narrow")
    count = len(pieces)
    full = jnp.zeros((count, *pieces[0].shape), pieces[0].dtype)
    for s, piece in enumerate(pieces):
        full = lax.dynamic_update_index_in_dim(full, piece, (level - s) % count, 0)
    return full


def scatter_core(keep, give):
    arrived = wide_xor(give, 1)
    return {i: [(keep, i), (arrived, i)] for i in range(keep.shape[0])}


def block_of(term):
    array, i = term
    return array[i].astype(single)


def blocks_of(places):
    array, numbers = places[0][0], [i for _, i in places]
    step = numbers[1] - numbers[0] if len(numbers) > 1 else 1
    if numbers == list(range(numbers[0], numbers[-1] + 1, step)):
        return array[numbers[0] : numbers[-1] + 1 : step].astype(single)
    return jnp.stack([array[i] for i in numbers]).astype(single)


def scatter_hop(terms, bit):
    low = bit >> 1
    sent = [i for i in terms if i & low]
    outgoing = sum(blocks_of([t[n] for t in (terms[i] for i in sent)]) for n in range(len(terms[sent[0]])))
    outgoing = outgoing.astype(bfloat)
    incoming = wide_xor(outgoing, bit)
    kept = {i: [*terms[i], (incoming, sent.index(i | low))] for i in terms if not i & low}
    return kept, outgoing


TILE = 256


def lasting(micros):
    return pl.CostEstimate(flops=int(micros * 1.1e9), bytes_accessed=1000, transcendentals=0)


def col_tiles(width):
    return [(at, min(TILE, width - at)) for at in range(0, width, TILE)]


def expert_body(wide_count, narrow_count, capacity, width, column, first, last, idx, *refs):
    refs = list(refs)
    take = lambda count: [refs.pop(0) for _ in range(count)]
    pieces = take(wide_count)
    shared_weights = take(1) if width else []
    norm_parts, (dy_all,) = take(narrow_count), take(1)
    if first:
        router_slots, slot_bias = take(2)
    else:
        gates, ranks = take(2)
    earlier_q = take(EXP_DEV - 1) if last else []
    sums_in = [] if first else take(2)
    keep, give, q_ref = take(3)
    if first:
        gates, ranks = take(2)
    sums_out = take(1 + narrow_count) if last else take(2)
    (w, stage, norm, dy, out_acc, grad_acc, rows, dy_rows, grad_rows, pre, act, grad_pre, sel, sel_t, gate, q_acc, turned) = take(17)
    if width:
        sw, s_stage, s_act, s_pre = take(4)
    if first:
        (rank_cols,) = take(1)
    if last:
        q_cols, q_low = take(2)
    sems = refs.pop(0)
    assert not refs
    me, slot, level = idx[0], idx[1], idx[2]
    part = norm_parts[0].shape[0]
    total = part * narrow_count
    shard = D // wide_count
    blocks = total // MB_TOK

    def row_of(r):
        return pl.multiple_of((me ^ r) * shard, 16)

    def slot_row(ref, number, at):
        tile = ref[:, at : at + MB_TOK]
        mine = lax.broadcasted_iota(jnp.int32, tile.shape, 0) == number
        return jnp.sum(jnp.where(mine, tile, 0.0), axis=0, keepdims=True)

    expert_copies = [
        pltpu.make_async_copy(
            pieces[r].at[:, pl.ds(column, ECOLS)], w.at[pl.ds(row_of(r), shard), :], sems.at[0]
        )
        for r in range(wide_count)
    ]
    shared_copies = [pltpu.make_async_copy(ref, sw, sems.at[4]) for ref in shared_weights]

    def from_below(s):
        return lax.rem(level + (narrow_count - s), narrow_count)

    token_copies = []
    for s, src in enumerate(norm_parts):
        here = pl.ds(s * part, part)
        theirs = dy_all.at[from_below(s)]
        moves = [(src, norm.at[here, :]), (theirs.at[:, pl.ds(0, D)], dy.at[here, :])]
        if first:
            moves.append((theirs.at[:, pl.ds(D, LANES)], rank_cols.at[here, :]))
        token_copies += [pltpu.make_async_copy(*move, sems.at[2]) for move in moves]
    sum_copies = [
        pltpu.make_async_copy(src, dst, sems.at[3])
        for src, dst in zip(sums_in, (out_acc, grad_acc))
    ]
    for copy in token_copies + expert_copies + sum_copies + shared_copies:
        copy.start()
    for copy in token_copies:
        copy.wait()

    if first:
        for at in range(0, total, TILE):
            logits = dot(norm[at : at + TILE, :], router_slots[...]) + slot_bias[...]
            exp_logits = jnp.exp(logits - jnp.max(logits, axis=-1, keepdims=True))
            probs = exp_logits / jnp.sum(exp_logits, axis=-1, keepdims=True)
            gates[:, at : at + TILE] = probs.T[: gates.shape[0], :]
            numbers = rank_cols[at : at + TILE, :].astype(single)
            ranks[:, at : at + TILE] = numbers.T[: gates.shape[0], :]
    if True:
        for b in range(blocks):
            rank_row = slot_row(ranks, slot, b * MB_TOK)
            gate_row = slot_row(gates, slot, b * MB_TOK)
            place_in = lax.broadcasted_iota(jnp.int32, (capacity, MB_TOK), 0).astype(single)
            hit = jnp.where(place_in == rank_row, 1.0, 0.0)
            here = pl.ds(b * capacity, capacity)
            gate_col = jnp.sum(hit * gate_row, axis=1, keepdims=True)
            gate[here, :] = jnp.broadcast_to(gate_col, (capacity, LANES))
            hit_low = hit.astype(bfloat)
            sel[here, :] = hit_low
            sel_t[pl.ds(b * MB_TOK, MB_TOK), :] = hit.T.astype(bfloat)
            tokens_here = pl.ds(b * MB_TOK, MB_TOK)
            rows[here, :] = dot(hit_low, norm[tokens_here, :]).astype(bfloat)
            picked = dot(hit_low, dy[tokens_here, :])
            dy_rows[here, :] = picked.astype(bfloat)
            grad_rows[here, :] = (gate_col * picked).astype(bfloat)
        for copy in expert_copies:
            copy.wait()

        @pl.loop(0, 2 * FF // TILE)
        def _(j):
            cols = pl.ds(pl.multiple_of(j * TILE, TILE), TILE)
            pre[:, cols] = dot(rows[...], w[:, cols])

        @pl.loop(0, rows.shape[0] // 32)
        def _(i):
            here = pl.ds(pl.multiple_of(i * 32, 32), 32)
            gate_pre, up_pre = pre[here, :FF], pre[here, FF:]
            sigma = jax.nn.sigmoid(gate_pre)
            silu = gate_pre * sigma
            act[here, :] = (silu * up_pre).astype(bfloat)
            pre[here, :FF] = up_pre * sigma * (1.0 + gate_pre * (1.0 - sigma))
            pre[here, FF:] = silu

        for copy in sum_copies:
            copy.wait()
        q_acc[...] = jnp.zeros_like(q_acc)

        def add_up(acc, tile, cols, fresh):
            for b in range(blocks):
                tokens_here = pl.ds(b * MB_TOK, MB_TOK)
                term = dot(sel_t[tokens_here, :], tile[b * capacity : (b + 1) * capacity, :])
                if fresh:
                    acc[tokens_here, cols] = term
                else:
                    acc[tokens_here, cols] += term

        @pl.loop(0, D // TILE)
        def _(j):
            cols = pl.ds(pl.multiple_of(j * TILE, TILE), TILE)
            out = dot(act[...], w[cols, 2 * FF :], NT).astype(bfloat).astype(single)
            product = out * dy_rows[:, cols].astype(single)
            q_acc[...] += product[:, :LANES] + product[:, LANES:]
            tile = (out * gate[:, :1]).astype(bfloat)
            add_up(out_acc, tile, cols, first)

        q_col = jnp.sum(q_acc[...], axis=1, keepdims=True)
        for b in range(blocks):
            here = slice(b * capacity, (b + 1) * capacity)
            q_ref[0:1, b * MB_TOK : (b + 1) * MB_TOK] = jnp.sum(
                sel[here, :].astype(single) * q_col[here], axis=0, keepdims=True
            )
        for at, n in col_tiles(FF):
            grad_act = dot(grad_rows[...], w[:, 2 * FF + at : 2 * FF + at + n])
            grad_pre[:, at : at + n] = (grad_act * pre[:, at : at + n]).astype(bfloat)
            grad_pre[:, FF + at : FF + at + n] = (
                grad_act * pre[:, FF + at : FF + at + n]
            ).astype(bfloat)

        @pl.loop(0, D // TILE)
        def _(j):
            cols = pl.ds(pl.multiple_of(j * TILE, TILE), TILE)
            tile = dot(grad_pre[...], w[cols, : 2 * FF], NT).astype(bfloat)
            add_up(grad_acc, tile, cols, first)

    if width:
        for copy in shared_copies:
            copy.wait()

        @pl.loop(0, total // TILE)
        def _(i):
            here = pl.ds(pl.multiple_of(i * TILE, TILE), TILE)
            gate_pre = dot(norm[here, :], sw[:, :width])
            up_pre = dot(norm[here, :], sw[:, width : 2 * width])
            sigma = jax.nn.sigmoid(gate_pre)
            silu = gate_pre * sigma
            s_act[here, :] = (silu * up_pre).astype(bfloat)
            grad_act = dot(dy[here, :], sw[:, 2 * width :])
            s_pre[here, :width] = (
                grad_act * up_pre * sigma * (1.0 + gate_pre * (1.0 - sigma))
            ).astype(bfloat)
            s_pre[here, width:] = (grad_act * silu).astype(bfloat)
            for at, n in col_tiles(D):
                cols = slice(at, at + n)
                out_acc[here, cols] += dot(s_act[here, :], sw[cols, 2 * width :], NT)
                grad_acc[here, cols] += dot(s_pre[here, :], sw[cols, : 2 * width], NT)

        @pl.loop(0, D // TILE)
        def _(j):
            cols = pl.ds(pl.multiple_of(j * TILE, TILE), TILE)
            s_stage[cols, : 2 * width] = dot(norm[:, cols], s_pre[...], TN).astype(bfloat)
            s_stage[cols, 2 * width :] = dot(dy[:, cols], s_act[...], TN).astype(bfloat)

    waiting = []
    if last:
        slots = EXP_DEV * narrow_count
        number = lax.broadcasted_iota(jnp.int32, (LANES, MB_TOK), 0)
        for b in range(blocks):
            tokens_here = slice(b * MB_TOK, (b + 1) * MB_TOK)
            table = jnp.zeros((LANES, MB_TOK), single)
            for e, ref in enumerate([*earlier_q, q_ref]):
                row = ref[0:1, tokens_here]
                high = row.astype(bfloat).astype(single)
                mine = slot - (EXP_DEV - 1) + e
                table = jnp.where(number == mine, high, table)
                table = jnp.where(number == slots + mine, row - high, table)
            q_cols[tokens_here, :] = table.T
        q_low[...] = q_cols[...].astype(bfloat)
        for s in range(narrow_count):
            here = pl.ds(s * part, part)
            waiting.append(
                pltpu.make_async_copy(
                    (q_low if s else q_cols).at[here, :],
                    sums_out[1 + s].at[:, pl.ds(D, LANES)],
                    sems.at[3],
                )
            )
            waiting[-1].start()
    if not last:
        for src, dst in zip((out_acc, grad_acc), sums_out):
            waiting.append(pltpu.make_async_copy(src, dst, sems.at[7]))
            waiting[-1].start()
    else:
        for acc, low in ((grad_acc, dy), (out_acc, norm)):
            for s in range(narrow_count):
                here = pl.ds(s * part, part)
                if acc is grad_acc:
                    target = sums_out[1 + s].at[:, pl.ds(0, D)]
                else:
                    target = sums_out[0].at[from_below(s)]
                source = low
                if s == 0 and acc is grad_acc:
                    source = acc
                else:

                    @pl.loop(0, part // 32)
                    def _(i):
                        some = pl.ds(pl.multiple_of(s * part + i * 32, 32), 32)
                        low[some, :] = acc[some, :].astype(bfloat)

                waiting.append(pltpu.make_async_copy(source.at[here, :], target, sems.at[7]))
                waiting[-1].start()
    if width:
        for r in range(wide_count):
            waiting.append(
                pltpu.make_async_copy(
                    s_stage.at[pl.ds(row_of(r), shard), :],
                    (give if r & 1 else keep).at[r // 2, :, pl.ds(ECOLS, 3 * width)],
                    sems.at[6],
                )
            )
            waiting[-1].start()
    if True:

        @pl.loop(0, D // TILE)
        def _(j):
            cols = pl.ds(pl.multiple_of(j * TILE, TILE), TILE)
            turned[...] = rows[:, cols].T

            @pl.loop(0, 2 * FF // TILE)
            def _(k):
                out_cols = pl.ds(pl.multiple_of(k * TILE, TILE), TILE)
                stage[cols, out_cols] = dot(turned[...], grad_pre[:, out_cols]).astype(bfloat)

            turned[...] = grad_rows[:, cols].T
            for at, n in col_tiles(FF):
                stage[cols, 2 * FF + at : 2 * FF + at + n] = dot(
                    turned[...], act[:, at : at + n]
                ).astype(bfloat)

    for r in range(wide_count):
        waiting.append(
            pltpu.make_async_copy(
                stage.at[pl.ds(row_of(r), shard), :],
                (give if r & 1 else keep).at[r // 2, :, pl.ds(0, ECOLS)],
                sems.at[5],
            )
        )
        waiting[-1].start()
    for copy in waiting:
        copy.wait()


def expert_call(pieces, column, shared_weights, tokens, gating, earlier_q, sums, index, capacity, last):
    wide_count = len(pieces)
    norm_parts, dy_all = tokens
    narrow_count = len(norm_parts)
    shard = D // wide_count
    part = norm_parts[0].shape[0]
    slots = EXP_DEV * narrow_count
    total = part * narrow_count
    count_rows = total // MB_TOK * capacity
    first = sums is None
    width = shared_weights[0].shape[1] // 3 if shared_weights else 0
    grads = lambda cols: jax.ShapeDtypeStruct((wide_count // 2, shard, cols), bfloat)
    if last:
        sum_shapes = [jax.ShapeDtypeStruct((narrow_count, part, D), bfloat)] + [
            jax.ShapeDtypeStruct((part, D + LANES), bfloat if s else single)
            for s in range(narrow_count)
        ]
    else:
        sum_shapes = [jax.ShapeDtypeStruct((total, D), single)] * 2
    any_space = pl.BlockSpec(memory_space=pl.ANY)
    vmem = pl.BlockSpec(memory_space=pltpu.VMEM)
    operands = [*pieces, *shared_weights, *norm_parts, dy_all]
    specs = [any_space] * len(operands)
    operands += [*gating, *earlier_q]
    specs += [vmem] * (len(operands) - len(specs))
    gate_shapes = [jax.ShapeDtypeStruct((slots, total), single)] * 2 if first else []
    if not first:
        operands += list(sums)
        specs += [any_space] * 2
    scratch = [
        pltpu.VMEM((D, ECOLS), bfloat),
        pltpu.VMEM((D, ECOLS), bfloat),
        pltpu.VMEM((total, D), bfloat),
        pltpu.VMEM((total, D), bfloat),
        pltpu.VMEM((total, D), single),
        pltpu.VMEM((total, D), single),
        pltpu.VMEM((count_rows, D), bfloat),
        pltpu.VMEM((count_rows, D), bfloat),
        pltpu.VMEM((count_rows, D), bfloat),
        pltpu.VMEM((count_rows, 2 * FF), single),
        pltpu.VMEM((count_rows, FF), bfloat),
        pltpu.VMEM((count_rows, 2 * FF), bfloat),
        pltpu.VMEM((count_rows, MB_TOK), bfloat),
        pltpu.VMEM((total, capacity), bfloat),
        pltpu.VMEM((count_rows, LANES), single),
        pltpu.VMEM((count_rows, LANES), single),
        pltpu.VMEM((TILE, count_rows), bfloat),
    ]
    if width:
        scratch += [
            pltpu.VMEM((D, 3 * width), bfloat),
            pltpu.VMEM((D, 3 * width), bfloat),
            pltpu.VMEM((total, width), bfloat),
            pltpu.VMEM((total, 2 * width), bfloat),
        ]
    if first:
        scratch.append(pltpu.VMEM((total, LANES), bfloat))
    if last:
        scratch += [pltpu.VMEM((total, LANES), single), pltpu.VMEM((total, LANES), bfloat)]
    scratch.append(pltpu.SemaphoreType.DMA((8,)))
    keep, give, q_row, *rest = pl.pallas_call(
        functools.partial(
            expert_body, wide_count, narrow_count, capacity, width, column, first, last
        ),
        out_shape=[
            grads(ECOLS + 3 * width),
            grads(ECOLS + 3 * width),
            jax.ShapeDtypeStruct((1, total), single),
            *gate_shapes,
            *sum_shapes,
        ],
        in_specs=[pl.BlockSpec(memory_space=pltpu.SMEM)] + specs,
        out_specs=[any_space] * 2
        + [vmem] * (1 + len(gate_shapes))
        + [any_space] * len(sum_shapes),
        scratch_shapes=scratch,
        compiler_params=pltpu.CompilerParams(vmem_limit_bytes=60 * 2**20),
        cost_estimate=lasting(36 + 8 * (width > 0)),
    )(index, *operands)
    if first:
        gating = [rest.pop(0), rest.pop(0)]
    return (keep, give), q_row, gating, rest


RATES = dict(zip(("attention_in", "attention_out", "shared_in", "shared_out", "router", "gains", "experts_in", "experts_out"), STEP_RATES))


def nesterov(grad, master, moment, average, rate):
    moment_new = MOMENTUM_DECAY * moment + grad
    master_new = master - rate * (grad + MOMENTUM_DECAY * moment_new)
    average_new = AVERAGE_DECAY * average + (1.0 - AVERAGE_DECAY) * master_new
    return moment_new, average_new, master_new


def expert_update_body(term_count, rates, *refs):
    terms = refs[:term_count]
    states = refs[term_count : term_count + 6]
    moment_in, state_in, moment_out, state_out = refs[-4:]
    read = lambda ref, cols: (ref[0, :, cols] if len(ref.shape) == 3 else ref[:, cols]).astype(single)
    for at, n, which, moment_ref, state_ref in (
        (0, 2 * FF, 0, moment_in, state_in),
        (2 * FF, FF, 3, moment_out, state_out),
    ):
        grad = sum(read(t, slice(at, at + n)) for t in terms)
        master, moment, average = (ref[0] for ref in states[which : which + 3])
        moment_ref[0], state_ref[0, 0], state_ref[1, 0] = nesterov(
            grad, master, moment, average, rates[which // 3]
        )


def expert_update(terms, states, held, expert, rates):
    rows = states[0].shape[1]
    tile = 80 if rows % 80 == 0 else rows
    specs, operands = [], []
    for array, block in terms:
        specs.append(pl.BlockSpec((1, tile, ECOLS), lambda i, block=block: (block, i, 0)))
        operands.append(array)
    for number, state in enumerate(states):
        width = 2 * FF if number < 3 else FF
        specs.append(pl.BlockSpec((1, tile, width), lambda i: (expert, i, 0)))
        operands.append(state)
    shapes, out_specs = [], []
    for width in (2 * FF, FF):
        shapes.append(jax.ShapeDtypeStruct((EXP_DEV, rows, width), single))
        out_specs.append(pl.BlockSpec((1, tile, width), lambda i: (expert, i, 0)))
        shapes.append(jax.ShapeDtypeStruct((2, EXP_DEV, rows, width), single))
        out_specs.append(pl.BlockSpec((2, 1, tile, width), lambda i: (0, expert, i, 0)))
    aliases = {}
    if held is not None:
        aliases = {len(operands) + k: k for k in range(4)}
        operands += held
        specs += [pl.BlockSpec(memory_space=pl.ANY)] * 4
    return pl.pallas_call(
        functools.partial(expert_update_body, len(terms), rates),
        grid=(rows // tile,),
        out_shape=shapes,
        in_specs=specs,
        out_specs=out_specs,
        input_output_aliases=aliases,
        compiler_params=pltpu.CompilerParams(vmem_limit_bytes=48 * 2**20),
        cost_estimate=lasting(5),
    )(*operands)


def dense_update_body(rates, own, come, *refs):
    states, outs = refs[:6], refs[6:]
    moment_in, state_in, moment_out, state_out, tail = outs
    for at, n, which, moment_ref, state_ref in (
        (0, 3 * D, 0, moment_in, state_in),
        (3 * D, D, 3, moment_out, state_out),
    ):
        cols = slice(at, at + n)
        grad = own[:, cols].astype(single) + come[:, cols].astype(single)
        master, moment, average = (ref[...] for ref in states[which : which + 3])
        moment_ref[...], state_ref[0], state_ref[1] = nesterov(
            grad, master, moment, average, rates[which // 3]
        )
    tail[...] = own[:, 4 * D :].astype(single) + come[:, 4 * D :].astype(single)


def dense_update(own, come, states, rates):
    rows = own.shape[0]
    out = lambda *shape: jax.ShapeDtypeStruct(shape, single)
    vmem = pl.BlockSpec(memory_space=pltpu.VMEM)
    return pl.pallas_call(
        functools.partial(dense_update_body, rates),
        out_shape=[
            out(rows, 3 * D),
            out(2, rows, 3 * D),
            out(rows, D),
            out(2, rows, D),
            out(rows, LANES),
        ],
        in_specs=[vmem] * 8,
        out_specs=[vmem] * 5,
        compiler_params=pltpu.CompilerParams(vmem_limit_bytes=48 * 2**20),
    )(own, come, *states)


def ring_gather(piece):
    pieces = [piece]
    for _ in range(lax.axis_size("narrow") - 1):
        pieces.append(ring(pieces[-1]))
    return pieces


def ring_scatter(parts):
    total = parts[1].astype(bfloat)
    for step in range(2, lax.axis_size("narrow")):
        total = (ring(total).astype(single) + parts[step].astype(single)).astype(bfloat)
    return parts[0], ring(total)


def pack_copies(w, lefts, rights, me, sem):
    shard = lefts[0].shape[0]
    cut = lefts[0].shape[1]
    copies = []
    for r, (left, right) in enumerate(zip(lefts, rights)):
        here = pl.ds(pl.multiple_of((me ^ r) * shard, 16), shard)
        copies.append(pltpu.make_async_copy(left, w.at[here, pl.ds(0, cut)], sem))
        copies.append(pltpu.make_async_copy(right, w.at[here, pl.ds(cut, ACOLS - cut)], sem))
    return copies


def turn(vectors, cosines, sines):
    return vectors * cosines + pltpu.roll(vectors, HEAD_DIM // 2, 1) * sines


def head_cols(part, head):
    return pl.ds(pl.multiple_of(part * D + head * HEAD_DIM, LANES), HEAD_DIM)


def row_probs(queries, keys_rot, bias):
    scores = dot(queries, keys_rot, NT) * HEAD_DIM ** (-0.5) + bias
    exp_scores = jnp.exp(scores - jnp.max(scores, axis=-1, keepdims=True))
    return exp_scores / jnp.sum(exp_scores, axis=-1, keepdims=True)


def attention_forward_body(wide_count, routed, idx, *refs):
    refs = list(refs)
    take = lambda count: [refs.pop(0) for _ in range(count)]
    lefts, rights = take(wide_count), take(wide_count)
    x, cosines, sines, bias, perm, slot_bias = take(6)
    hidden, second_norm, first_norm, qkv, attended, router_probs, router_slots, gain_rows = take(8)
    w, projected, sem = refs
    copies = pack_copies(w, lefts, rights, idx[0], sem)
    for copy in copies:
        copy.start()
    for copy in copies:
        copy.wait()
    tail = w[:, 4 * D :]
    gain_rows[...] = tail.astype(single).T[routed : routed + 2, :]
    rows_in = x[...].astype(single)
    first_norm[...] = (rows_in * rms_scale(rows_in) * gain_rows[0:1, :]).astype(bfloat)

    @pl.loop(0, 3 * D // TILE)
    def _(j):
        cols = pl.ds(pl.multiple_of(j * TILE, TILE), TILE)
        projected[:, cols] = dot(first_norm[...], w[:, cols])

    @pl.loop(0, HEADS)
    def _(head):
        for part in range(2):
            cols = head_cols(part, head)
            qkv[:, cols] = turn(projected[:, cols], cosines[...], sines[...]).astype(bfloat)
        cols = head_cols(2, head)
        qkv[:, cols] = projected[:, cols].astype(bfloat)
        for b in range(MB):
            here = slice(b * MB_TOK, (b + 1) * MB_TOK)
            probs = row_probs(
                qkv[here, head_cols(0, head)], qkv[here, head_cols(1, head)], bias[here, :]
            ).astype(bfloat)
            attended[here, head_cols(0, head)] = dot(probs, qkv[here, cols]).astype(bfloat)

    for at, n in col_tiles(D):
        hidden[:, at : at + n] = rows_in[:, at : at + n] + dot(
            attended[...], w[:, 3 * D + at : 3 * D + at + n]
        )
    rows_mid = hidden[...]
    second_norm[...] = (rows_mid * rms_scale(rows_mid) * gain_rows[1:2, :]).astype(bfloat)
    router_slots[...] = dot(tail, perm[...]).astype(bfloat)
    logits = dot(second_norm[...], router_slots[...]) + slot_bias[...]
    exp_logits = jnp.exp(logits - jnp.max(logits, axis=-1, keepdims=True))
    probs = exp_logits / jnp.sum(exp_logits, axis=-1, keepdims=True)
    router_probs[...] = probs


def attention_backward_body(wide_count, routed, slots, idx, *refs):
    refs = list(refs)
    take = lambda count: [refs.pop(0) for _ in range(count)]
    lefts, rights = take(wide_count), take(wide_count)
    x, cosines, sines, bias, perm = take(5)
    hidden, second_norm, first_norm, qkv, attended, router_probs, gain_rows = take(7)
    dy, second_own, second_come = take(3)
    keep_left, give_left, keep_right, give_right, input_grad = take(5)
    w, stage, grad_second, grad_hidden, grad_branch, grad_attended, grad_projected, turned, tail_rows, sems = refs
    me = idx[0]
    copies = pack_copies(w, lefts, rights, me, sems.at[0])
    for copy in copies:
        copy.start()
    for copy in copies:
        copy.wait()
    probs = router_probs[...]
    q = second_own[:, D:] + second_come[:, D:].astype(single)
    q = q + pltpu.roll(q, LANES - slots, 1)
    grad_logits = probs * (q - jnp.sum(probs * q, axis=-1, keepdims=True))
    high = grad_logits.astype(bfloat)
    rest = (grad_logits - high.astype(single)).astype(bfloat)
    router_slots = dot(w[:, 4 * D :], perm[...]).astype(bfloat)
    for at, n in col_tiles(D):
        cols = slice(at, at + n)
        grad_second[:, cols] = (
            second_own[:, cols]
            + second_come[:, cols].astype(single)
            + dot(high, router_slots[cols, :], NT)
            + dot(rest, router_slots[cols, :], NT)
        )
    tail_rows[...] = jnp.zeros_like(tail_rows)
    rows_mid = hidden[...]
    scale = rms_scale(rows_mid)
    normed = rows_mid * scale
    weighted = grad_second[...] * gain_rows[1:2, :]
    tail_rows[1:2, :] = jnp.sum(grad_second[...] * normed, axis=0, keepdims=True)
    grad_hidden[...] = dy[...].astype(single) + scale * (
        weighted - normed * jnp.mean(weighted * normed, axis=-1, keepdims=True)
    )
    grad_branch[...] = grad_hidden[...].astype(bfloat)

    @pl.loop(0, D // TILE)
    def _(j):
        cols = pl.ds(pl.multiple_of(j * TILE, TILE), TILE)
        grad_attended[:, cols] = dot(grad_branch[...], w[cols, 3 * D : 4 * D], NT).astype(bfloat)
        turned[...] = attended[:, cols].T

        for at, n in col_tiles(D):
            stage[cols, 3 * D + at : 3 * D + at + n] = dot(
                turned[...], grad_branch[:, at : at + n]
            ).astype(bfloat)

    @pl.loop(0, HEADS)
    def _(head):
        for b in range(MB):
            here = slice(b * MB_TOK, (b + 1) * MB_TOK)
            queries = qkv[here, head_cols(0, head)]
            keys_rot = qkv[here, head_cols(1, head)]
            values = qkv[here, head_cols(2, head)]
            probs = row_probs(queries, keys_rot, bias[here, :])
            grad_out = grad_attended[here, head_cols(0, head)]
            grad_values = dot(probs.astype(bfloat), grad_out, TN)
            grad_probs = dot(grad_out, values, NT)
            grad_scores = probs * (
                grad_probs - jnp.sum(probs * grad_probs, axis=-1, keepdims=True)
            )
            grad_scores = grad_scores.astype(bfloat)
            grad_queries = dot(grad_scores, keys_rot) * HEAD_DIM ** (-0.5)
            grad_keys = dot(grad_scores, queries, TN) * HEAD_DIM ** (-0.5)
            for part, grad in enumerate((grad_queries, grad_keys)):
                grad_projected[here, head_cols(part, head)] = turn(
                    grad, cosines[here, :], -sines[here, :]
                ).astype(bfloat)
            grad_projected[here, head_cols(2, head)] = grad_values.astype(bfloat)

    @pl.loop(0, D // TILE)
    def _(j):
        cols = pl.ds(pl.multiple_of(j * TILE, TILE), TILE)
        grad_second[:, cols] = dot(grad_projected[...], w[cols, : 3 * D], NT)
        turned[...] = first_norm[:, cols].T

        @pl.loop(0, 3 * D // TILE)
        def _(k):
            out_cols = pl.ds(pl.multiple_of(k * TILE, TILE), TILE)
            stage[cols, out_cols] = dot(turned[...], grad_projected[:, out_cols]).astype(bfloat)

    rows_in = x[...].astype(single)
    scale = rms_scale(rows_in)
    normed = rows_in * scale
    weighted = grad_second[...] * gain_rows[0:1, :]
    tail_rows[0:1, :] = jnp.sum(grad_second[...] * normed, axis=0, keepdims=True)
    input_grad[...] = (
        grad_hidden[...]
        + scale * (weighted - normed * jnp.mean(weighted * normed, axis=-1, keepdims=True))
    ).astype(bfloat)
    high_expert = dot(high, perm[...], NT).astype(bfloat)
    rest_expert = dot(rest, perm[...], NT).astype(bfloat)
    lane = lax.broadcasted_iota(jnp.int32, (TILE, LANES), 1)
    for at, n in col_tiles(D):
        gain_cols = tail_rows[:, at : at + n].T
        router_cols = dot(second_norm[:, at : at + n], high_expert, TN) + dot(
            second_norm[:, at : at + n], rest_expert, TN
        )
        stage[at : at + n, 4 * D :] = (
            router_cols
            + jnp.where(lane == routed, gain_cols[:, 0:1], 0.0)
            + jnp.where(lane == routed + 1, gain_cols[:, 1:2], 0.0)
        ).astype(bfloat)
    shard = D // wide_count
    cut = split_cols(ACOLS)
    copies = []
    for r in range(wide_count):
        here = pl.ds(pl.multiple_of((me ^ r) * shard, 16), shard)
        for refs_out, at, n in (
            ((keep_left, give_left), 0, cut),
            ((keep_right, give_right), cut, ACOLS - cut),
        ):
            copies.append(
                pltpu.make_async_copy(
                    stage.at[here, pl.ds(at, n)], refs_out[r & 1].at[r // 2], sems.at[1]
                )
            )
    for copy in copies:
        copy.start()
    for copy in copies:
        copy.wait()


def attention_forward(lefts, rights, operands, index, routed, slots):
    wide_count = len(lefts)
    part = operands[0].shape[0]
    out = jax.ShapeDtypeStruct
    vmem = pl.BlockSpec(memory_space=pltpu.VMEM)
    any_space = pl.BlockSpec(memory_space=pl.ANY)
    return pl.pallas_call(
        functools.partial(attention_forward_body, wide_count, routed),
        out_shape=[
            out((part, D), single),
            out((part, D), bfloat),
            out((part, D), bfloat),
            out((part, 3 * D), bfloat),
            out((part, D), bfloat),
            out((part, LANES), single),
            out((D, LANES), bfloat),
            out((2, D), single),
        ],
        in_specs=[pl.BlockSpec(memory_space=pltpu.SMEM)]
        + [any_space] * (2 * wide_count)
        + [vmem] * len(operands),
        out_specs=[vmem] * 8,
        scratch_shapes=[
            pltpu.VMEM((D, ACOLS), bfloat),
            pltpu.VMEM((part, 3 * D), single),
            pltpu.SemaphoreType.DMA,
        ],
        compiler_params=pltpu.CompilerParams(vmem_limit_bytes=60 * 2**20),
        cost_estimate=lasting(24),
    )(index, *lefts, *rights, *operands)


def attention_backward(lefts, rights, operands, index, routed, slots):
    wide_count = len(lefts)
    part = operands[0].shape[0]
    out = jax.ShapeDtypeStruct
    vmem = pl.BlockSpec(memory_space=pltpu.VMEM)
    any_space = pl.BlockSpec(memory_space=pl.ANY)
    cut = split_cols(ACOLS)
    shard = D // wide_count
    grads = lambda cols: out((wide_count // 2, shard, cols), bfloat)
    return pl.pallas_call(
        functools.partial(attention_backward_body, wide_count, routed, slots),
        out_shape=[
            grads(cut),
            grads(cut),
            grads(ACOLS - cut),
            grads(ACOLS - cut),
            out((part, D), bfloat),
        ],
        in_specs=[pl.BlockSpec(memory_space=pltpu.SMEM)]
        + [any_space] * (2 * wide_count)
        + [vmem] * len(operands),
        out_specs=[any_space] * 4 + [vmem],
        scratch_shapes=[
            pltpu.VMEM((D, ACOLS), bfloat),
            pltpu.VMEM((D, ACOLS), bfloat),
            pltpu.VMEM((part, D), single),
            pltpu.VMEM((part, D), single),
            pltpu.VMEM((part, D), bfloat),
            pltpu.VMEM((part, D), bfloat),
            pltpu.VMEM((part, 3 * D), bfloat),
            pltpu.VMEM((TILE, part), bfloat),
            pltpu.VMEM((8, D), single),
            pltpu.SemaphoreType.DMA((2,)),
        ],
        compiler_params=pltpu.CompilerParams(vmem_limit_bytes=60 * 2**20),
        cost_estimate=lasting(50),
    )(index, *lefts, *rights, *operands)


def local(
    block_in,
    cotangent,
    routes,
    seq_ids,
    slot_order,
    attention_in,
    attention_in_moment,
    attention_in_average,
    attention_out,
    attention_out_moment,
    attention_out_average,
    shared_in,
    shared_in_moment,
    shared_in_average,
    shared_out,
    shared_out_moment,
    shared_out_average,
    router,
    router_moment,
    router_average,
    gains,
    gains_moment,
    gains_average,
    experts_in,
    experts_in_moment,
    experts_in_average,
    experts_out,
    experts_out_moment,
    experts_out_average,
):
    wide_count = lax.axis_size("wide")
    narrow_count = lax.axis_size("narrow")
    level = lax.axis_index("narrow")
    slots = EXP_DEV * narrow_count
    routed = slots - 1
    capacity = (MB_TOK * TOPK * 8 // (7 * slots) + 7) // 8 * 8
    tokens = MB * MB_TOK * wide_count * narrow_count
    own_tokens = MB * MB_TOK
    rows_dense = D // (wide_count * narrow_count)
    rows_plane = D // wide_count
    quarter = FF // narrow_count
    shared_width = (quarter + LANES - 1) // LANES * LANES

    pad_small = jnp.zeros((rows_dense, LANES - routed - 2), bfloat)
    attention_pack = jnp.concatenate(
        [
            attention_in.astype(bfloat),
            attention_out.astype(bfloat),
            router.astype(bfloat),
            gains.T.astype(bfloat),
            pad_small,
        ],
        axis=1,
    )
    late_in, late_out, late_shared_in, late_shared_out = lax.optimization_barrier(
        (experts_in, experts_out, shared_in, shared_out, attention_pack)
    )[:4]
    expert_pack = [
        jnp.concatenate(
            [part for e in (h, h + 2) for part in (late_in[e], late_out[e].T)], axis=1
        ).astype(bfloat)
        for h in range(2)
    ]
    orders = [chip_bits(), chip_bits()[::-1]]
    early = [first_hops({0: expert_pack[e]}, orders[e][0]) for e in range(2)]

    attention_parts = [attention_pack]
    for _ in range(narrow_count - 1):
        attention_parts.append(ring(attention_parts[-1]))
    cut = split_cols(ACOLS)
    attention_pieces = [
        place([p[:, :cut] for p in attention_parts]).reshape(rows_plane, cut),
        place([p[:, cut:] for p in attention_parts]).reshape(rows_plane, ACOLS - cut),
    ]

    route_hot = (routes[..., None] == jnp.arange(routed, dtype=jnp.int32)).astype(single).sum(axis=2)
    slot_hot_of_expert = (
        slot_order[:routed, None] == jnp.arange(slots, dtype=jnp.int32)
    ).astype(single)
    chosen = jnp.dot(route_hot.reshape(own_tokens, routed), slot_hot_of_expert)
    positions = jnp.arange(MB_TOK, dtype=jnp.int32)
    below = (positions[:, None] > positions[None, :]).astype(bfloat)
    ranks = jnp.einsum(
        "tu,bue->bte", below, chosen.reshape(MB, MB_TOK, slots).astype(bfloat), preferred_element_type=single
    ).reshape(own_tokens, slots)
    rank_own = jnp.where(chosen > 0.5, ranks, -1.0).astype(bfloat)
    grad_out = cotangent.reshape(own_tokens, D)
    token_pack = jnp.concatenate(
        [grad_out, jnp.pad(rank_own, ((0, 0), (0, LANES - slots)))], axis=1
    )
    dy_all = lax.all_gather(after(token_pack, attention_parts[-1]), "narrow")
    early_done = [p for pieces in early for p in pieces.values()]
    attention_chips = [
        gather_chips(p, order, first_hops({0: p}, order[0]), early_done)
        for p, order in zip(attention_pieces, orders)
    ]
    attention_halves = [core_hops(chips) for chips in attention_chips]

    shared_pack = jnp.concatenate([late_shared_in, late_shared_out.T], axis=1).astype(bfloat)
    shared_pack = shared_pack.reshape(rows_dense, 3, narrow_count, quarter)
    shared_pack = jnp.pad(shared_pack, ((0, 0), (0, 0), (0, 0), (0, shared_width - quarter)))
    shared_pack = shared_pack.transpose(2, 0, 1, 3).reshape(
        narrow_count, rows_dense, 3 * shared_width
    )
    shared_piece = lax.all_to_all(
        shared_pack, "narrow", split_axis=0, concat_axis=0, tiled=True
    ).reshape(rows_plane, 3 * shared_width)

    first_last = [chips[max(chips)] for chips in attention_chips]
    own_hops = [
        first_hops({0: after(expert_pack[h], *first_last)}, bit)
        for h in range(2)
        for bit in orders[h][1:2]
    ]
    shared_weights = lax.all_gather(shared_piece, "wide", axis=0, tiled=True)

    wide_index = after(lax.axis_index("wide").reshape(1), dy_all, shared_weights)
    perm = jnp.pad(
        slot_hot_of_expert, ((0, LANES - routed), (0, LANES - slots))
    ).astype(bfloat)
    slot_bias = jnp.where(jnp.sum(perm.astype(single), axis=0, keepdims=True) > 0.0, 0.0, MASKED)
    half_dim = HEAD_DIM // 2
    freqs = jnp.exp(jnp.arange(half_dim, dtype=single) * (-2.0 * math.log(10000.0) / HEAD_DIM))
    angles = (positions - seq_ids).reshape(own_tokens, 1).astype(single) * freqs
    cosines, sines = jnp.cos(angles), jnp.sin(angles)
    cosines = jnp.concatenate([cosines, cosines], axis=1)
    sines = jnp.concatenate([-sines, sines], axis=1)
    allowed = (seq_ids[:, :, None] == seq_ids[:, None, :]) & (
        positions[None, None, :] <= positions[None, :, None]
    )
    bias = jnp.where(allowed, 0.0, MASKED).reshape(own_tokens, MB_TOK)
    rows_in = block_in.reshape(own_tokens, D)
    tables = (cosines, sines, bias, perm)
    hidden, second_norm, first_norm, qkv, attended, router_probs, router_slots, gain_rows = attention_forward(
        *attention_halves, (rows_in, *tables, slot_bias), wide_index, routed, slots
    )

    norm_parts = ring_gather(second_norm)
    expert_pieces = []
    for h in range(2):
        chips = {0: expert_pack[h], **early[h]}
        swapped = core_hops({r: after(p, second_norm) for r, p in chips.items()}, pairs=True)
        for number, bit in enumerate(orders[h][1:]):
            source = {r: after(p, second_norm) for r, p in chips.items() if r or number}
            if number == 0:
                chips.update(own_hops[h])
            chips.update(first_hops(source, bit))
        late = {r: after(p, norm_parts[-1]) for r, p in chips.items() if r not in swapped}
        swapped.update(core_hops(late, pairs=True))
        expert_pieces.append([p for r in sorted(swapped) for p in swapped[r]])
    tokens_in = (norm_parts, dy_all)
    gating = [router_slots, slot_bias]
    sums, q_rows = None, []
    terms, bits_left = [], [order[::-1] for order in orders] * 2

    def hop(e):
        bit, bits_left[e] = bits_left[e][0], bits_left[e][1:]
        terms[e], outgoing = scatter_hop(terms[e], bit)
        return outgoing

    for e in range(EXP_DEV):
        index = jnp.stack([lax.axis_index("wide"), level * EXP_DEV + e, level])
        if e == EXP_DEV - 2:
            index = after(index, *[hop(n) for n in range(2)])
        if e == EXP_DEV - 1:
            index = after(index, *[hop(n) for n in range(2)])
        grads, q_row, gating, sums = expert_call(
            expert_pieces[e % 2],
            e // 2 * ECOLS,
            [shared_weights] if e == 2 else [],
            tokens_in,
            gating,
            q_rows if e == EXP_DEV - 1 else [],
            sums,
            index,
            capacity,
            e == EXP_DEV - 1,
        )
        terms.append(scatter_core(*grads))
        q_rows.append(q_row)
    out_parts, grad_parts = sums[0], sums[1:]
    second_own, second_come = ring_scatter(grad_parts)
    sent = [hop(e) for e in range(2) for _ in range(len(bits_left[e]))]
    sent += [hop(e) for e in range(2, EXP_DEV)]
    wide_index = after(wide_index, *sent)
    *attention_grads, input_grad = attention_backward(
        *attention_halves,
        (
            rows_in,
            *tables,
            hidden,
            second_norm,
            first_norm,
            qkv,
            attended,
            router_probs,
            gain_rows,
            grad_out,
            second_own,
            second_come,
        ),
        wide_index,
        routed,
        slots,
    )
    input_grad = input_grad.reshape(MB, MB_TOK, D)
    attention_terms = [
        scatter_core(*attention_grads[:2]),
        scatter_core(*attention_grads[2:]),
    ]

    out_come = lax.psum_scatter(after(out_parts, second_come), "narrow", scatter_dimension=0)
    block_out = hidden + out_come.astype(single)
    block_out = block_out.astype(bfloat).reshape(MB, MB_TOK, D)

    first_sent, second_sent = [], []
    for level_bit in range(len(orders[0])):
        for h in range(2):
            attention_terms[h], outgoing = scatter_hop(attention_terms[h], orders[h][::-1][level_bit])
            (second_sent if level_bit else first_sent).append(outgoing)
    attention_share = jnp.concatenate(
        [sum(block_of(t) for t in attention_terms[h][0]) for h in range(2)], axis=1
    ).astype(bfloat)
    attention_share = attention_share.reshape(narrow_count, rows_dense, ACOLS)
    attention_own, attention_come = ring_scatter(
        [
            lax.dynamic_index_in_dim(attention_share, (level - s) % narrow_count, 0, False)
            for s in range(narrow_count)
        ]
    )
    for e in range(2, EXP_DEV):
        for _ in range(len(bits_left[e])):
            terms[e] = {i: [(after(a, *second_sent), n) for a, n in ts] for i, ts in terms[e].items()}
            hop(e)
    shared_terms = [after(array[block, :, ECOLS:], *second_sent) for array, block in terms[2][0]]
    shared_share = sum(term.astype(single) for term in shared_terms)
    shared_share = shared_share.astype(bfloat).reshape(narrow_count, rows_dense, 3 * shared_width)
    shared_share = lax.all_to_all(
        shared_share, "narrow", split_axis=0, concat_axis=0, tiled=True
    ).reshape(narrow_count, rows_dense, 3, shared_width)[..., :quarter]
    shared_share = shared_share.transpose(1, 2, 0, 3).reshape(rows_dense, 3 * FF).astype(single)

    base_rate = 1.0 / math.sqrt(tokens)
    rate = {name: value * base_rate for name, value in RATES.items()}
    turn_out = lambda array: array.transpose(0, 2, 1)
    states = (
        experts_in,
        experts_in_moment,
        experts_in_average,
        turn_out(experts_out),
        turn_out(experts_out_moment),
        turn_out(experts_out_average),
    )
    held = None
    for e in range(EXP_DEV):
        held = expert_update(
            [(after(array, *first_sent, *([out_come] if e == 2 else [])), block) for array, block in terms[e][0]],
            states,
 held, e, (rate["experts_in"], rate["experts_out"])
        )
    experts_in_new, experts_in_state, experts_out_new, experts_out_state = held
    attention_in_new, attention_in_state, attention_out_new, attention_out_state, tail = dense_update(
        attention_own,
        attention_come,
        (
            attention_in,
            attention_in_moment,
            attention_in_average,
            attention_out,
            attention_out_moment,
            attention_out_average,
        ),
        (rate["attention_in"], rate["attention_out"]),
    )

    def plain(name, grad, *old):
        moment_new, average_new, master_new = nesterov(grad, *old, rate[name])
        return moment_new, jnp.stack([average_new, master_new])

    shared_in_new, shared_in_state = plain(
        "shared_in", shared_share[:, : 2 * FF], shared_in, shared_in_moment, shared_in_average
    )
    shared_out_new, shared_out_state = plain(
        "shared_out", shared_share[:, 2 * FF :].T, shared_out, shared_out_moment, shared_out_average
    )
    router_new, router_state = plain(
        "router", tail[:, :routed], router, router_moment, router_average
    )
    gains_new, gains_state = plain(
        "gains", tail[:, routed : routed + 2].T, gains, gains_moment, gains_average
    )
    return (
        block_out,
        input_grad,
        attention_in_new,
        attention_out_new,
        shared_in_new,
        shared_out_new,
        router_new,
        gains_new,
        experts_in_new,
        turn_out(experts_out_new),
        attention_in_state,
        attention_out_state,
        shared_in_state,
        shared_out_state,
        router_state,
        gains_state,
        experts_in_state,
        experts_out_state.transpose(0, 1, 3, 2),
    )


def solution(mesh):
    both = ("wide", "narrow")
    token = P(None, both, None)
    rows = P(both, None)
    cols = P(None, both)
    weight_specs = [rows, rows, rows, cols, rows, cols, P("narrow", "wide", None), P("narrow", None, "wide")]
    in_specs = (token, token, token, P(None, both), P()) + tuple(
        spec for spec in weight_specs for _ in range(3)
    )
    out_specs = (token, token, *weight_specs, *(P(None, *spec) for spec in weight_specs))
    return jax.shard_map(local, mesh=mesh, in_specs=in_specs, out_specs=out_specs, check_vma=False)
```
